512 devices in a mesh: section: 8 (over y_hi, core), dp: 64 (over x, z, y_lo).
Axes of the slice: x: 4, y: 8 (y_hi: 4, y_lo: 2; y = y_hi * 2 + y_lo), z: 8, core: 2. Of those that a mesh axis runs over, the one named last changes fastest.
Arguments:
- inputs: bfloat16 [2, 4096, 4096], P(None, 'dp'), may hold values from -6 to 6
- cotangent: bfloat16 [2, 4096, 4096], P(None, 'dp'), may hold values from -6 to 6
- doc_lengths: int32 [2, 64, 2], P(None, 'dp'), may hold values from 1 to 48, 64 in all within a row
- norm_gain: bfloat16 [8, 4096], P('section'), may hold values from 0.25 to 1.75
- w_qkv: bfloat16 [8, 4096, 192], P('section', 'dp'), may hold values from -0.09375 to 0.09375
- w_out: bfloat16 [8, 64, 4096], P('section', None, 'dp'), may hold values from -0.75 to 0.75
Outputs:
- grad_qkv: float32 [8, 4096, 192], P('section', 'dp')
- grad_out: float32 [8, 64, 4096], P('section', None, 'dp')
The draws below stay inside these ranges and needn't reach their ends.
Inputs may be any that keep to these rules, and one draw needn't show every extreme that they name: `doc_lengths`: each row's 2 lengths add up to 64.
All inputs are finite; a program needn't handle non-finite values.
Results may differ from the reference program's by a relative error of at most 0.025.
Values may be sent and summed in bfloat16 or wider, within the bound.
A program may use at most 64 MiB of HBM per device.

```python
import math
import jax
import jax.numpy as jnp
import numpy as np
from jax import lax

D = 4096
HD = 64
MBTOK = 64
MB = 2
DOCS = 2
SECTIONS = 8
TOKENS = 4096
N_SECTION = 8
N_DP = 64


def steps_of(stream_key, extent, shards, least, largest):
    level, own = 1.0, jax.random.fold_in(stream_key, 6)
    for axis_at, blocks in shards:
        draws = jnp.exp(jax.random.uniform(jax.random.fold_in(own, axis_at), (blocks,), jnp.float32, least / len(shards), largest / len(shards)))
        level = level * jnp.repeat(draws, extent[axis_at] // blocks).reshape([-1 if axis == axis_at else 1 for axis in range(len(extent))])
    return level


def profile(count, total, limit, lean):
    loads = [(1 << 20) // math.isqrt(grade ** lean) + 1 for grade in range(2, count + 1)]
    rest, given = total - limit - (count - 1), [1] * (count - 1)
    while rest > 0:
        free = [i for i in range(count - 1) if given[i] < limit]
        mass, left = sum([loads[i] for i in free]), rest
        for i in free:
            more = min(limit - given[i], max(1, left * loads[i] // mass), rest)
            given[i] = given[i] + more
            rest = rest - more
    return np.array([limit] + given)


def ragged(stream_key, count, total, bound, slope):
    if count == 2:
        one = jax.random.randint(stream_key, (), max(1, total - bound), min(bound, total - 1) + 1)
        return jnp.stack([one, total - one])
    sizes = jnp.asarray(profile(count, total, bound, slope), jnp.int32)
    pairs = (count - 1) // 2
    source_of, sink = sizes[1:1 + 2 * pairs:2], sizes[2:2 + 2 * pairs:2]
    margin = jnp.minimum(source_of - 1, bound - sink)
    moved = jax.random.randint(jax.random.fold_in(stream_key, 1), (pairs,), 0, 1 << 20) % (margin + 1)
    sizes = sizes.at[1:1 + 2 * pairs:2].set(source_of - moved).at[2:2 + 2 * pairs:2].set(sink + moved)
    return sizes[jax.random.permutation(jax.random.fold_in(stream_key, 2), count)]


def bell_draw(rng, extent, width, reach, pieces=(), kind=jnp.bfloat16):
    values = width * jax.random.normal(rng, extent, jnp.float32)
    if pieces:
        values = values * steps_of(rng, extent, pieces, -0.22, 0.18)
    return jnp.clip(values, -reach, reach).astype(kind)


def setup_inputs(seed: int = 0) -> dict:
    streams_of = jax.random.split(jax.random.key(seed), 7)
    inputs = bell_draw(streams_of[0], (MB, TOKENS, D), 1.0, 6.0, ((1, 64),))
    cotangent = bell_draw(streams_of[1], (MB, TOKENS, D), 1.0, 6.0, ((1, 64),))
    doc_lengths = jax.vmap(lambda own: ragged(own, DOCS, MBTOK, MBTOK * 3 // 4, 2))(jax.random.split(streams_of[2], MB * N_DP)).reshape((MB, N_DP, DOCS)).astype(jnp.int32)
    norm_gain = jnp.clip(1.0 + 0.15 * jax.random.normal(streams_of[3], (SECTIONS, D), jnp.float32), 0.25, 1.75).astype(jnp.bfloat16)
    w_qkv = bell_draw(streams_of[4], (SECTIONS, D, 3 * HD), D ** -0.5, 0.09375, ((0, 8), (1, 64)))
    w_out = bell_draw(streams_of[5], (SECTIONS, HD, D), HD ** -0.5, 0.75, ((0, 8), (2, 64)))
    return dict(inputs=inputs, cotangent=cotangent, doc_lengths=doc_lengths, norm_gain=norm_gain, w_qkv=w_qkv, w_out=w_out)


def segments_of(lengths, count):
    ends = jnp.cumsum(lengths).astype(jnp.int32)
    position = jnp.arange(count, dtype=jnp.int32)
    return lax.optimization_barrier(jnp.sum((position[:, None] >= ends[None, :]).astype(jnp.int32), axis=1)).astype(jnp.int32)

def layer(x, gain, w_qkv, w_out, seg):
    head = w_out.shape[0]
    x_wide = x.astype(jnp.float32)
    scale = lax.rsqrt(lax.optimization_barrier(jnp.mean(x_wide * x_wide, axis=-1, keepdims=True)) + 1e-05)
    normed = (x_wide * scale * gain.astype(jnp.float32)).astype(jnp.bfloat16)
    qkv = jnp.dot(normed, w_qkv, preferred_element_type=jnp.float32).astype(jnp.bfloat16)
    query = qkv[:, :head]
    keys = qkv[:, head:2 * head]
    values = qkv[:, 2 * head:]
    scores = jnp.dot(query, keys.T, preferred_element_type=jnp.float32) * head ** (-0.5)
    rows = jnp.arange(x.shape[0], dtype=jnp.int32)
    allowed = (seg[:, None] == seg[None, :]) & (rows[:, None] >= rows[None, :])
    scores = jnp.where(allowed, scores, -1e+30)
    probs = jax.nn.softmax(scores, axis=-1).astype(jnp.bfloat16)
    attended = jnp.dot(probs, values, preferred_element_type=jnp.float32).astype(jnp.bfloat16)
    return (x_wide + jnp.dot(attended, w_out, preferred_element_type=jnp.float32)).astype(jnp.bfloat16)

def reference(inputs, cotangent, doc_lengths, norm_gain, w_qkv, w_out):
    blocks = inputs.reshape(MB, N_DP, MBTOK, D)
    cot_blocks = cotangent.reshape(MB, N_DP, MBTOK, D)
    segs = jax.vmap(jax.vmap(lambda lens: segments_of(lens, MBTOK)))(doc_lengths)

    def run(x, cot, seg):
        saved = []
        for level in range(N_SECTION):
            saved.append(x)
            x = layer(x, norm_gain[level], w_qkv[level], w_out[level], seg)
        grad_in = cot
        qkv_list = []
        out_list = []
        for level in reversed(range(N_SECTION)):
            gain = norm_gain[level]
            _, pull = jax.vjp(lambda a, b, c: layer(a, gain, b, c, seg), saved[level], w_qkv[level], w_out[level])
            grad_in, grad_q, grad_o = pull(grad_in)
            qkv_list.insert(0, grad_q)
            out_list.insert(0, grad_o)
        return (jnp.stack(qkv_list), jnp.stack(out_list))
    total_qkv = jnp.zeros(w_qkv.shape, jnp.float32)
    total_out = jnp.zeros(w_out.shape, jnp.float32)
    for micro in range(MB):
        grad_q, grad_o = jax.vmap(run)(blocks[micro], cot_blocks[micro], segs[micro])
        total_qkv = total_qkv + lax.optimization_barrier(jnp.sum(grad_q.astype(jnp.float32), axis=0))
        total_out = total_out + lax.optimization_barrier(jnp.sum(grad_o.astype(jnp.float32), axis=0))
    return (total_qkv, total_out)
```

```python
import functools

import jax
import jax.numpy as jnp
from jax import lax
from jax.experimental import pallas as pl
from jax.experimental.pallas import tpu as pltpu
from jax.sharding import PartitionSpec as P

MESH = pl.DeviceIdType.MESH
F32, BF16 = jnp.float32, jnp.bfloat16
SUB = 16


def nn(a, b):
    return jnp.dot(a, b, preferred_element_type=F32)


def nt(a, b):
    return lax.dot_general(a, b, (((1,), (1,)), ((), ())), preferred_element_type=F32)


def tn(a, b):
    return lax.dot_general(a, b, (((0,), (0,)), ((), ())), preferred_element_type=F32)


def kernel(
    nc, nx, nz, rows,
    inp, cot, lens, wg, out,
    W, xin, cin, X, DY, QK, KK, VV, PR, ATT, SC, SD,
    es, er, bs, br, G, SR, H, XR, H2, ZR, H3, YR, FS, OB,
    in_sem, s1_s, s1_r, y_s, y_r, z_s, z_r, x_s, x_r, c_s, c_r,
    e_s, e_r, b_s, b_r, rc_s, rc_r, rx_s, rx_r, rz_s, rz_r, ry_s, ry_r, f_s, f_r,
):
    layers = 2 * nc
    dps = nx * nz * 2
    local = SUB * dps
    width = local * nc
    zrows, xrows = 2 * SUB, 2 * SUB * nz
    s, d = lax.axis_index("section"), lax.axis_index("dp")
    c, k = lax.div(s, 2), lax.rem(s, 2)
    x, z, y = lax.div(d, 2 * nz), lax.rem(lax.div(d, 2), nz), lax.rem(d, 2)

    def at(start, size):
        return pl.ds(pl.multiple_of(start, SUB), size)

    def section_peer(o):
        return lax.rem(s + o, layers)

    def chip_peer(o):
        return (2 * lax.rem(c + o, nc) + k, d)

    def x_peer(o):
        return lax.rem(x + o, nx)

    def z_peer(o):
        return lax.rem(z + o, nz)

    def dp_of(px, pz, py):
        return (px * nz + pz) * 2 + py

    sibling = (2 * c + 1 - k, d)
    y_partner = (s, dp_of(x, z, 1 - y))

    def send(src, dst, send_sem, recv_sem, device):
        pltpu.make_async_remote_copy(
            src_ref=src, dst_ref=dst, send_sem=send_sem, recv_sem=recv_sem,
            device_id=device, device_id_type=MESH,
        ).start()

    def wait(ref, sem):
        pltpu.make_async_copy(ref, ref, sem).wait()

    load_x = pltpu.make_async_copy(inp.at[k], xin, in_sem.at[0])
    load_c = pltpu.make_async_copy(cot.at[k], cin, in_sem.at[1])
    own = pltpu.make_async_copy(
        wg.at[k, at(SUB * c, SUB)], W.at[k, s, at(SUB * d, SUB)], in_sem.at[2]
    )
    load_x.start()
    load_c.start()
    own.start()

    barrier = pltpu.get_barrier_semaphore()
    peers = [(section_peer(o), d) for o in range(1, layers)]
    peers += [(s, dp_of(x_peer(o), z, y)) for o in range(1, nx)]
    peers += [(s, dp_of(x, z_peer(o), y)) for o in range(1, nz)]
    peers += [y_partner]
    for peer in peers:
        pl.semaphore_signal(barrier, inc=1, device_id=peer, device_id_type=MESH)
    pl.semaphore_wait(barrier, len(peers))

    for o in range(1, layers):
        t = section_peer(o)
        tc, tk = lax.div(t, 2), lax.rem(t, 2)
        send(
            wg.at[tk, at(SUB * tc, SUB)], W.at[tk, s, at(SUB * d, SUB)],
            s1_s, s1_r, (t, d),
        )

    load_x.wait()
    load_c.wait()
    grain = min(8, dps)
    big, small = grain * SUB * nc, grain * SUB
    at_row = lax.broadcasted_iota(jnp.int32, (big, small), 0)
    at_lane = lax.broadcasted_iota(jnp.int32, (big, small), 1)
    wanted = lax.div(at_lane, SUB) * (SUB * nc) + lax.rem(at_lane, SUB) + SUB * c
    pick = jnp.where(at_row == wanted, 1.0, 0.0).astype(BF16)
    for m in range(dps // grain):
        X[0, :, m * small : (m + 1) * small] = nn(
            xin[:, m * big : (m + 1) * big], pick
        ).astype(BF16)
        DY[layers - 1, :, m * small : (m + 1) * small] = nn(
            cin[:, m * big : (m + 1) * big], pick
        ).astype(BF16)

    own.wait()
    wait(W.at[0, 0, pl.ds(0, SUB * (layers - 1))], s1_r)
    mine = W.at[k, :, at(SUB * d, SUB)]
    send(mine, mine, y_s, y_r, y_partner)
    wait(mine, y_r)

    def z_gather(l):
        block = W.at[k, l, at(zrows * (x * nz + z), zrows)]
        for o in range(1, nz):
            send(block, block, z_s, z_r.at[l], (s, dp_of(x, z_peer(o), y)))

    def x_gather(l):
        if nz > 1:
            wait(W.at[0, 0, pl.ds(0, zrows * (nz - 1))], z_r.at[l])
        block = W.at[k, l, at(xrows * x, xrows)]
        for o in range(1, nx):
            send(block, block, x_s, x_r.at[l], (s, dp_of(x_peer(o), z, y)))

    def core_gather(l):
        if nx > 1:
            wait(W.at[0, 0, pl.ds(0, xrows * (nx - 1))], x_r.at[l])
        send(W.at[k, l], W.at[k, l], c_s, c_r.at[l], sibling)

    row = lax.broadcasted_iota(jnp.int32, (rows, rows), 0)
    col = lax.broadcasted_iota(jnp.int32, (rows, rows), 1)
    first = lens[k, 0]
    allowed = ((row < first) == (col < first)) & (row >= col)
    lane = lax.broadcasted_iota(jnp.int32, (rows, 128), 1)
    low = lane < 64

    def both(l):
        return jnp.concatenate([W[0, l], W[1, l]], axis=1)

    def forward(l, between):
        slot = lax.rem(l, 2)
        wait(W.at[0, 0], c_r.at[l])
        xb = X[l]
        part = nn(xb, both(l))
        wide = xb.astype(F32)
        square = jnp.sum(wide * wide, axis=1, keepdims=True)
        upper = square.astype(BF16).astype(F32)
        es[slot, :, :128] = part[:, :128].astype(BF16)
        tail = jnp.where(lane < 96, upper, square - upper)
        es[slot, :, 128:] = jnp.where(low, part[:, 128:], tail).astype(BF16)
        for o in range(1, nc):
            send(es.at[slot], er.at[slot, o - 1], e_s.at[slot], e_r.at[slot], chip_peer(o))
        between(l)
        t0, t1 = part[:, :128], part[:, 128:]
        if nc > 1:
            wait(er.at[slot], e_r.at[slot])
            for o in range(nc - 1):
                t0 = t0 + er[slot, o, :, :128].astype(F32)
                more = er[slot, o, :, 128:].astype(F32)
                t1 = t1 + more
                square = square + more[:, 64:65] + more[:, 96:97]
            wait(er.at[slot], e_s.at[slot])
        scale = lax.rsqrt(square * (1.0 / width) + 1e-05)
        q = t0 * scale
        kk = pltpu.roll(q, 64, 1).astype(BF16)
        vv = pltpu.roll(jnp.where(low, t1 * scale, 0.0), 64, 1).astype(BF16)
        scores = nt(jnp.where(low, q, 0.0).astype(BF16), kk) * 0.125
        scores = jnp.where(allowed, scores, -1e30)
        top = jnp.max(scores, axis=1, keepdims=True)
        e = jnp.exp(scores - top)
        p = e / jnp.sum(e, axis=1, keepdims=True)
        att = nn(p.astype(BF16), vv).astype(BF16)
        QK[l] = q.astype(BF16)
        KK[l] = kk
        VV[l] = vv
        PR[l] = p
        ATT[l] = att
        SC[l] = jnp.broadcast_to(scale, (rows, 128))

        @pl.when(l < layers - 1)
        def _():
            X[l + 1] = (X[l].astype(F32) + nt(att, W[1, l])).astype(BF16)

    def ahead(l):
        @pl.when(l + 3 < layers)
        def _():
            z_gather(l + 3)

        @pl.when(l + 2 < layers)
        def _():
            x_gather(l + 2)

        @pl.when(l + 1 < layers)
        def _():
            core_gather(l + 1)

    z_gather(0)
    if layers > 1:
        z_gather(1)
    x_gather(0)
    if layers > 2:
        z_gather(2)
    if layers > 1:
        x_gather(1)
    core_gather(0)

    def forward_step(l, carry):
        forward(l, ahead)
        return carry

    lax.fori_loop(0, layers, forward_step, 0)

    def grads(l):
        left = jnp.concatenate([X[l], DY[l]], axis=0)
        att = ATT[l]
        right = jnp.concatenate(
            [
                jnp.concatenate([SD[l, 0], SD[l, 1]], axis=1),
                jnp.concatenate([jnp.zeros_like(att), att], axis=1),
            ],
            axis=0,
        )
        g = tn(left, right)
        G[l, 0] = g[:, :128].astype(BF16)
        G[l, 1] = g[:, 128:].astype(BF16)
        send(G.at[l, 1 - k], SR.at[l], rc_s, rc_r.at[l], sibling)

    def x_scatter(l):
        wait(SR.at[l], rc_r.at[l])
        H[l] = (G[l, k].astype(F32) + SR[l].astype(F32)).astype(BF16)
        for o in range(1, nx):
            px = x_peer(o)
            send(
                H.at[l, at(xrows * px, xrows)], XR.at[l, o - 1],
                rx_s, rx_r.at[l], (s, dp_of(px, z, y)),
            )

    def z_scatter(l):
        total = H[l, at(xrows * x, xrows)].astype(F32)
        if nx > 1:
            wait(XR.at[l], rx_r.at[l])
            for o in range(nx - 1):
                total = total + XR[l, o].astype(F32)
        H2[l] = total.astype(BF16)
        for o in range(1, nz):
            pz = z_peer(o)
            send(
                H2.at[l, at(zrows * pz, zrows)], ZR.at[l, o - 1],
                rz_s, rz_r.at[l], (s, dp_of(x, pz, y)),
            )

    def y_scatter(l):
        total = H2[l, at(zrows * z, zrows)].astype(F32)
        if nz > 1:
            wait(ZR.at[l], rz_r.at[l])
            for o in range(nz - 1):
                total = total + ZR[l, o].astype(F32)
        H3[l] = total.astype(BF16)
        send(H3.at[l, at(SUB * (1 - y), SUB)], YR.at[l], ry_s, ry_r.at[l], y_partner)

    def finish(l):
        wait(YR.at[l], ry_r.at[l])
        FS[l] = H3[l, at(SUB * y, SUB)].astype(F32) + YR[l].astype(F32)

    def staged(l, behind, stage):
        @pl.when((l + behind >= 0) & (l + behind < layers))
        def _():
            stage(l + behind)

    def backward_step(step, carry):
        l = layers - 1 - step
        slot = lax.rem(step, 2)

        @pl.when(l >= 0)
        def _():
            part = nn(DY[l], W[1, l])
            bs[slot] = part.astype(BF16)
            for o in range(1, nc):
                send(bs.at[slot], br.at[slot, o - 1], b_s.at[slot], b_r.at[slot], chip_peer(o))

        staged(l, 1, grads)
        staged(l, 2, x_scatter)
        staged(l, 3, z_scatter)
        staged(l, 4, y_scatter)
        staged(l, 5, finish)

        @pl.when(l >= 0)
        def _():
            total = bs[slot].astype(F32)
            if nc > 1:
                wait(br.at[slot], b_r.at[slot])
                for o in range(nc - 1):
                    total = total + br[slot, o].astype(F32)
                wait(br.at[slot], b_s.at[slot])
            da = jnp.where(low, 0.0, total).astype(BF16)
            vv, kk, p, scale = VV[l], KK[l], PR[l], SC[l]
            dp = nt(da, vv)
            ds = p * (dp - jnp.sum(p * dp, axis=1, keepdims=True)) * 0.125
            ds = ds.astype(BF16)
            dqk = jnp.where(low, nn(ds, kk), tn(ds, kk))
            dv = tn(p.astype(BF16), da)
            dot = dqk * QK[l].astype(F32) + dv * vv.astype(F32)
            dot = jnp.sum(dot, axis=1, keepdims=True)
            coef = scale[:, :1] * scale[:, :1] * dot * (1.0 / width)
            sd0 = (dqk * scale).astype(BF16)
            sd1 = (pltpu.roll(dv, 64, 1) * scale).astype(BF16)
            SD[l, 0] = sd0
            SD[l, 1] = sd1

            @pl.when(l > 0)
            def _():
                step_x = nt(jnp.concatenate([sd0, sd1], axis=1), both(l))
                DY[l - 1] = (
                    DY[l].astype(F32) + step_x - X[l].astype(F32) * coef
                ).astype(BF16)

        return carry

    lax.fori_loop(0, layers + 5, backward_step, 0)

    for o in range(1, layers):
        t = section_peer(o)
        send(FS.at[t], OB.at[k, at(SUB * c, SUB)], f_s, f_r, (t, d))
    OB[k, at(SUB * c, SUB)] = FS[s]
    wait(FS.at[pl.ds(0, layers - 1)], f_r)
    out[...] = OB[...]

    wait(W.at[0, 0, pl.ds(0, SUB * (layers - 1))], s1_s)
    wait(mine, y_s)
    if nz > 1:
        for o in range(1, nz):
            wait(W.at[0, :, pl.ds(0, zrows)], z_s)
            wait(H2.at[:, pl.ds(0, zrows)], rz_s)
    if nx > 1:
        for o in range(1, nx):
            wait(W.at[0, :, pl.ds(0, xrows)], x_s)
            wait(H2, rx_s)
    wait(W.at[0], c_s)
    wait(H, rc_s)
    wait(YR, ry_s)
    wait(FS.at[pl.ds(0, layers - 1)], f_s)


def body(nc, nx, nz, inputs, cotangent, doc_lengths, norm_gain, w_qkv, w_out):
    rows, width = inputs.shape[1:]
    layers, dps = 2 * nc, nx * nz * 2
    local = SUB * dps
    grain = SUB * nc
    d = lax.axis_index("dp")
    gain = lax.dynamic_slice(norm_gain[0], (d * grain,), (grain,)).astype(F32)[:, None]
    wq = (w_qkv[0].astype(F32) * gain).astype(BF16)
    wg = jnp.concatenate([wq, w_out[0].T], axis=1)
    wg = jnp.stack([wg[:, :128], wg[:, 128:]])
    vmem = pl.BlockSpec(memory_space=pltpu.VMEM)
    anywhere = pl.BlockSpec(memory_space=pl.ANY)
    dma = pltpu.SemaphoreType.DMA
    xrows, zrows = 2 * SUB * nz, 2 * SUB
    sums = pl.pallas_call(
        functools.partial(kernel, nc, nx, nz, rows),
        out_shape=jax.ShapeDtypeStruct((2, grain, 128), F32),
        in_specs=[anywhere, anywhere, pl.BlockSpec(memory_space=pltpu.SMEM), vmem],
        out_specs=vmem,
        scratch_shapes=[
            pltpu.VMEM((2, layers, local, 128), BF16),
            pltpu.VMEM((rows, width), BF16),
            pltpu.VMEM((rows, width), BF16),
            pltpu.VMEM((layers, rows, local), BF16),
            pltpu.VMEM((layers, rows, local), BF16),
            pltpu.VMEM((layers, rows, 128), BF16),
            pltpu.VMEM((layers, rows, 128), BF16),
            pltpu.VMEM((layers, rows, 128), BF16),
            pltpu.VMEM((layers, rows, rows), F32),
            pltpu.VMEM((layers, rows, 128), BF16),
            pltpu.VMEM((layers, rows, 128), F32),
            pltpu.VMEM((layers, 2, rows, 128), BF16),
            pltpu.VMEM((2, rows, 256), BF16),
            pltpu.VMEM((2, max(nc - 1, 1), rows, 256), BF16),
            pltpu.VMEM((2, rows, 128), BF16),
            pltpu.VMEM((2, max(nc - 1, 1), rows, 128), BF16),
            pltpu.VMEM((layers, 2, local, 128), BF16),
            pltpu.VMEM((layers, local, 128), BF16),
            pltpu.VMEM((layers, local, 128), BF16),
            pltpu.VMEM((layers, max(nx - 1, 1), xrows, 128), BF16),
            pltpu.VMEM((layers, xrows, 128), BF16),
            pltpu.VMEM((layers, max(nz - 1, 1), zrows, 128), BF16),
            pltpu.VMEM((layers, zrows, 128), BF16),
            pltpu.VMEM((layers, SUB, 128), BF16),
            pltpu.VMEM((layers, SUB, 128), F32),
            pltpu.VMEM((2, grain, 128), F32),
            dma((3,)),
            dma, dma, dma, dma,
            dma, dma((layers,)), dma, dma((layers,)), dma, dma((layers,)),
            dma((2,)), dma((2,)), dma((2,)), dma((2,)),
            dma, dma((layers,)), dma, dma((layers,)),
            dma, dma((layers,)), dma, dma((layers,)),
            dma, dma,
        ],
        compiler_params=pltpu.CompilerParams(
            collective_id=0, has_side_effects=True, vmem_limit_bytes=50 * 2**20
        ),
        cost_estimate=pl.CostEstimate(
            flops=24 * layers * rows * local * 256,
            bytes_accessed=4 * rows * width,
            transcendentals=layers * rows * rows,
        ),
    )(inputs, cotangent, doc_lengths[:, 0, :], wg)
    full = jnp.concatenate([sums[0], sums[1]], axis=1)
    return ((full[:, :192] * gain)[None], full[:, 192:].T[None])


def solution(mesh, nx=4, nz=8):
    nc = mesh.shape["section"] // 2
    return jax.shard_map(
        functools.partial(body, nc, nx, nz),
        mesh=mesh,
        in_specs=(
            P(None, "dp", None),
            P(None, "dp", None),
            P(None, "dp", None),
            P("section", None),
            P("section", "dp", None),
            P("section", None, "dp"),
        ),
        out_specs=(P("section", "dp", None), P("section", None, "dp")),
        check_vma=False,
    )
```

```python
import functools

import jax
import jax.numpy as jnp
from jax import lax
from jax.experimental import pallas as pl
from jax.experimental.pallas import tpu as pltpu
from jax.sharding import PartitionSpec as P

MESH = pl.DeviceIdType.MESH
F32, BF16 = jnp.float32, jnp.bfloat16
SUB = 16


def nn(a, b):
    return jnp.dot(a, b, preferred_element_type=F32)


def nt(a, b):
    return lax.dot_general(a, b, (((1,), (1,)), ((), ())), preferred_element_type=F32)


def tn(a, b):
    return lax.dot_general(a, b, (((0,), (0,)), ((), ())), preferred_element_type=F32)


def kernel(
    nc, nx, nz, rows,
    inp, cot, lens, wg, out,
    W, xin, cin, X, DY, QK, KK, VV, PR, ATT, SC, SD, GM, UA,
    es, er, bs, br, gs, gr, G, SR, H, XR, H2, ZR, TALLY, TALLYB, FS, OB,
    in_sem, s1_s, s1_r, z_s, z_r, x_s, x_r, c_s, c_r,
    e_s, e_r, b_s, b_r, g_s, g_r, rc_s, rc_r, rx_s, rx_r, rz_s, rz_r, f_s, f_r,
):
    layers, pairs = 2 * nc, nc
    dps = nx * nz * 2
    local = SUB * dps
    width = local * nc
    zrows, xrows = 2 * SUB, 2 * SUB * nz
    s, d = lax.axis_index("section"), lax.axis_index("dp")
    c, k = lax.div(s, 2), lax.rem(s, 2)
    x, z, y = lax.div(d, 2 * nz), lax.rem(lax.div(d, 2), nz), lax.rem(d, 2)

    def at(start, size):
        return pl.ds(pl.multiple_of(start, SUB), size)

    def two(m):
        return pl.ds(2 * m, 2)

    def dp_of(px, pz, py):
        return (px * nz + pz) * 2 + py

    def far_first(n):
        return sorted(range(1, n), key=lambda o: -min(o, n - o))

    def column_peer(o):
        n = lax.rem(y * layers + s + o, 2 * layers)
        return lax.rem(n, layers), lax.div(n, layers)

    def chip_peer(o):
        return (2 * lax.rem(c + o, nc) + k, d)

    def x_peer(o):
        return lax.rem(x + o, nx)

    def z_peer(o):
        return lax.rem(z + o, nz)

    sibling = (2 * c + 1 - k, d)

    def send(src, dst, send_sem, recv_sem, device):
        pltpu.make_async_remote_copy(
            src_ref=src, dst_ref=dst, send_sem=send_sem, recv_sem=recv_sem,
            device_id=device, device_id_type=MESH,
        ).start()

    def wait(ref, sem):
        pltpu.make_async_copy(ref, ref, sem).wait()

    load_x = pltpu.make_async_copy(inp.at[k], xin, in_sem.at[0])
    load_c = pltpu.make_async_copy(cot.at[k], cin, in_sem.at[1])
    own = pltpu.make_async_copy(
        wg.at[k, at(SUB * c, SUB)], W.at[k, s, at(SUB * d, SUB)], in_sem.at[2]
    )
    load_x.start()
    load_c.start()
    own.start()

    barrier = pltpu.get_barrier_semaphore()
    peers = []
    for o in range(1, 2 * layers):
        t, ty = column_peer(o)
        peers += [(t, dp_of(x, z, ty))]
    peers += [(s, dp_of(x_peer(o), z, y)) for o in range(1, nx)]
    peers += [(s, dp_of(x, z_peer(o), y)) for o in range(1, nz)]
    for peer in peers:
        pl.semaphore_signal(barrier, inc=1, device_id=peer, device_id_type=MESH)
    grain = min(8, dps)
    big, small = grain * SUB * nc, grain * SUB
    at_row = lax.broadcasted_iota(jnp.int32, (big, small), 0)
    at_lane = lax.broadcasted_iota(jnp.int32, (big, small), 1)
    inside = at_lane & (SUB - 1)
    wanted = (at_lane - inside) * nc + inside + SUB * c
    pick = jnp.where(at_row == wanted, 1.0, 0.0).astype(BF16)

    def picked(source, m):
        return nn(source[:, m * big : (m + 1) * big], pick).astype(BF16)

    load_x.wait()
    for m in range(dps // grain):
        X[0, :, m * small : (m + 1) * small] = picked(xin, m)

    pl.semaphore_wait(barrier, len(peers))

    for o in range(1, 2 * layers):
        t, ty = column_peer(o)
        tc, tk = lax.div(t, 2), lax.rem(t, 2)
        send(
            wg.at[tk, at(SUB * tc, SUB)], W.at[tk, s, at(SUB * d, SUB)],
            s1_s, s1_r, (t, dp_of(x, z, ty)),
        )

    own.wait()
    columns = TALLYB.at[pl.ds(0, 2 * layers - 1)]
    wait(columns, s1_r)

    def z_gather(m):
        block = W.at[k, two(m), at(zrows * (x * nz + z), zrows)]
        for o in far_first(nz):
            send(block, block, z_s, z_r.at[m], (s, dp_of(x, z_peer(o), y)))

    def z_arrived(m):
        if nz > 1:
            wait(W.at[0, pl.ds(0, 2), pl.ds(0, zrows * (nz - 1))], z_r.at[m])

    def x_gather(m):
        block = W.at[k, two(m), at(xrows * x, xrows)]
        for o in far_first(nx):
            send(block, block, x_s, x_r.at[m], (s, dp_of(x_peer(o), z, y)))

    def x_arrived(m):
        if nx > 1:
            wait(W.at[0, pl.ds(0, 2), pl.ds(0, xrows * (nx - 1))], x_r.at[m])

    def core_gather(m):
        block = W.at[k, two(m)]
        send(block, block, c_s, c_r.at[m], sibling)

    def gamma(m):
        @pl.when(m > 0)
        def _():
            wait(W.at[0, pl.ds(0, 2)], c_r.at[m])

        a, b = 2 * m, 2 * m + 1
        right = jnp.concatenate([W[0, b], W[1, b], W[1, a]], axis=1)
        part = tn(W[1, a], right)[64:]
        gs[m] = part.astype(BF16)
        for o in far_first(nc):
            send(gs.at[m], gr.at[m, o - 1], g_s.at[m], g_r.at[m], chip_peer(o))

    def gamma_sum(m):
        total = gs[m].astype(F32)
        if nc > 1:
            wait(gr.at[m], g_r.at[m])
            for o in range(nc - 1):
                total = total + gr[m, o].astype(F32)
            wait(gr.at[m], g_s.at[m])
        GM[m, :64] = jnp.zeros((64, 384), BF16)
        GM[m, 64:] = total.astype(BF16)

    row = lax.broadcasted_iota(jnp.int32, (rows, rows), 0)
    col = lax.broadcasted_iota(jnp.int32, (rows, rows), 1)
    first = lens[k, 0]
    allowed = ((row < first) == (col < first)) & (row >= col)
    lane = lax.broadcasted_iota(jnp.int32, (rows, 128), 1)
    low = lane < 64

    def both(l):
        return jnp.concatenate([W[0, l], W[1, l]], axis=1)

    def attend(l, t0, t1, square):
        scale = lax.rsqrt(square * (1.0 / width) + 1e-05)
        q = t0 * scale
        kk = pltpu.roll(q, 64, 1).astype(BF16)
        vv = pltpu.roll(jnp.where(low, t1 * scale, 0.0), 64, 1).astype(BF16)
        scores = nt(jnp.where(low, q, 0.0).astype(BF16), kk) * 0.125
        scores = jnp.where(allowed, scores, -1e30)
        top = jnp.max(scores, axis=1, keepdims=True)
        e = jnp.exp(scores - top)
        p = e / jnp.sum(e, axis=1, keepdims=True)
        att = nn(p.astype(BF16), vv).astype(BF16)
        QK[l] = q.astype(BF16)
        KK[l] = kk
        VV[l] = vv
        PR[l] = p
        ATT[l] = att
        SC[l] = jnp.broadcast_to(scale, (rows, 128))
        return att

    def forward(m):
        slot = lax.rem(m, 2)
        a, b = 2 * m, 2 * m + 1
        xb = X[a]
        part = nn(xb, jnp.concatenate([both(a), both(b)], axis=1))
        wide = xb.astype(F32)
        square = jnp.sum(wide * wide, axis=1, keepdims=True)
        upper = square.astype(BF16).astype(F32)
        es[slot, :, :384] = part[:, :384].astype(BF16)
        tail = jnp.where(lane < 96, upper, square - upper)
        es[slot, :, 384:] = jnp.where(low, part[:, 384:], tail).astype(BF16)
        for o in far_first(nc):
            send(es.at[slot], er.at[slot, o - 1], e_s.at[slot], e_r.at[slot], chip_peer(o))
        between(m)
        gamma_sum(m)
        t = [part[:, 128 * i : 128 * (i + 1)] for i in range(4)]
        if nc > 1:
            wait(er.at[slot], e_r.at[slot])
            for o in range(nc - 1):
                for i in range(4):
                    t[i] = t[i] + er[slot, o, :, 128 * i : 128 * (i + 1)].astype(F32)
                more = er[slot, o, :, 384:].astype(F32)
                square = square + more[:, 64:65] + more[:, 96:97]
            wait(er.at[slot], e_s.at[slot])
        att = attend(a, t[0], t[1], square)
        u = nn(att, GM[m])
        into = jnp.where(low, 0.0, t[1])
        after = into + jnp.where(low, 0.0, u[:, 256:])
        UA[m] = after
        square = square + jnp.sum(att.astype(F32) * (into + after), axis=1, keepdims=True)
        last = attend(b, t[2] + u[:, :128], t[3] + u[:, 128:256], square)
        middle = (X[a].astype(F32) + nt(att, W[1, a])).astype(BF16)
        X[b] = middle

        @pl.when(m < pairs - 1)
        def _():
            X[b + 1] = (middle.astype(F32) + nt(last, W[1, b])).astype(BF16)

    def between(m):
        @pl.when(m == 0)
        def _():
            gamma(0)

        @pl.when(m + 2 < pairs)
        def _():
            z_arrived(m + 2)
            x_gather(m + 2)

        @pl.when(m + 3 < pairs)
        def _():
            z_gather(m + 3)

        @pl.when(m + 1 < pairs)
        def _():
            x_arrived(m + 1)
            core_gather(m + 1)
            gamma(m + 1)

    z_gather(0)
    load_c.wait()
    for m in range(dps // grain):
        DY[layers - 1, :, m * small : (m + 1) * small] = picked(cin, m)
    z_arrived(0)
    x_gather(0)
    if pairs > 1:
        z_gather(1)
        z_arrived(1)
        x_gather(1)
    if pairs > 2:
        z_gather(2)
    x_arrived(0)
    core_gather(0)
    wait(W.at[0, pl.ds(0, 2)], c_r.at[0])

    def forward_step(m, carry):
        forward(m)
        return carry

    lax.fori_loop(0, pairs, forward_step, 0)

    def grads(m):
        for l in (2 * m, 2 * m + 1):
            left = jnp.concatenate([X[l], DY[l]], axis=0)
            att = ATT[l]
            right = jnp.concatenate(
                [
                    jnp.concatenate([SD[l, 0], SD[l, 1]], axis=1),
                    jnp.concatenate([jnp.zeros_like(att), att], axis=1),
                ],
                axis=0,
            )
            g = tn(left, right)
            G[0, l] = g[:, :128].astype(BF16)
            G[1, l] = g[:, 128:].astype(BF16)
        send(G.at[1 - k, two(m)], SR.at[two(m)], rc_s, rc_r.at[m], sibling)

    def x_scatter(m):
        wait(SR.at[two(m)], rc_r.at[m])
        H[two(m)] = (G[k, two(m)].astype(F32) + SR[two(m)].astype(F32)).astype(BF16)
        for o in far_first(nx):
            px = x_peer(o)
            send(
                H.at[two(m), at(xrows * px, xrows)], XR.at[m, o - 1],
                rx_s, rx_r.at[m], (s, dp_of(px, z, y)),
            )

    def z_scatter(m):
        total = H[two(m), at(xrows * x, xrows)].astype(F32)
        if nx > 1:
            wait(XR.at[m], rx_r.at[m])
            for o in range(nx - 1):
                total = total + XR[m, o].astype(F32)
        H2[two(m)] = total.astype(BF16)
        for o in far_first(nz):
            pz = z_peer(o)
            send(
                H2.at[two(m), at(zrows * pz, zrows)], ZR.at[m, o - 1],
                rz_s, rz_r.at[m], (s, dp_of(x, pz, y)),
            )

    def finish(m):
        total = H2[two(m), at(zrows * z, zrows)].astype(F32)
        if nz > 1:
            wait(ZR.at[m], rz_r.at[m])
            for o in range(nz - 1):
                total = total + ZR[m, o].astype(F32)
        FS[two(m)] = total

    def staged(m, behind, stage):
        @pl.when((m + behind >= 0) & (m + behind < pairs))
        def _():
            stage(m + behind)

    def attend_back(l, da):
        da = jnp.where(low, 0.0, da).astype(BF16)
        vv, kk, p, scale = VV[l], KK[l], PR[l], SC[l]
        dp = nt(da, vv)
        ds = p * (dp - jnp.sum(p * dp, axis=1, keepdims=True)) * 0.125
        ds = ds.astype(BF16)
        dqk = jnp.where(low, nn(ds, kk), tn(ds, kk))
        dv = tn(p.astype(BF16), da)
        dot = dqk * QK[l].astype(F32) + dv * vv.astype(F32)
        dot = jnp.sum(dot, axis=1, keepdims=True)
        coef = scale[:, :1] * scale[:, :1] * dot * (1.0 / width)
        sd0 = (dqk * scale).astype(BF16)
        sd1 = (pltpu.roll(dv, 64, 1) * scale).astype(BF16)
        SD[l, 0] = sd0
        SD[l, 1] = sd1
        return jnp.concatenate([sd0, sd1], axis=1), coef

    def down(l, sd, coef):
        change = nt(sd, both(l)) - X[l].astype(F32) * coef
        DY[l - 1] = (DY[l].astype(F32) + change).astype(BF16)

    def backward_step(step, carry):
        m = pairs - 1 - step
        slot = lax.rem(step, 2)
        a, b = 2 * m, 2 * m + 1

        @pl.when(m >= 0)
        def _():
            part = nn(DY[b], jnp.concatenate([W[1, b], W[1, a]], axis=1))
            part = jnp.where(low, pltpu.roll(part[:, 128:], 64, 1), part[:, :128])
            bs[slot] = part.astype(BF16)
            for o in far_first(nc):
                send(bs.at[slot], br.at[slot, o - 1], b_s.at[slot], b_r.at[slot], chip_peer(o))

        staged(m, 1, grads)
        staged(m, 2, z_scatter)
        staged(m, 1, x_scatter)
        staged(m, 3, finish)

        @pl.when(m >= 0)
        def _():
            total = bs[slot].astype(F32)
            if nc > 1:
                wait(br.at[slot], b_r.at[slot])
                for o in range(nc - 1):
                    total = total + br[slot, o].astype(F32)
                wait(br.at[slot], b_s.at[slot])
            sd, coef = attend_back(b, total)
            other = nt(sd, GM[m, :, :256]) - UA[m] * coef
            down(b, sd, coef)
            sd, coef = attend_back(a, pltpu.roll(total, 64, 1) + other)

            @pl.when(m > 0)
            def _():
                down(a, sd, coef)

        return carry

    lax.fori_loop(0, pairs + 3, backward_step, 0)

    for o in range(1, 2 * layers):
        t, ty = column_peer(o)
        send(
            FS.at[t, at(SUB * ty, SUB)], OB.at[y, k, at(SUB * c, SUB)],
            f_s, f_r, (t, dp_of(x, z, ty)),
        )
    OB[y, k, at(SUB * c, SUB)] = FS[s, at(SUB * y, SUB)]
    wait_f = TALLY.at[pl.ds(0, 2 * layers - 1)]
    wait(wait_f, f_r)
    out[...] = OB[0] + OB[1]

    wait(columns, s1_s)
    if nz > 1:
        for o in range(1, nz):
            wait(W.at[0, :, pl.ds(0, zrows)], z_s)
            wait(H2.at[:, pl.ds(0, zrows)], rz_s)
    if nx > 1:
        for o in range(1, nx):
            wait(W.at[0, :, pl.ds(0, xrows)], x_s)
            wait(H2, rx_s)
    wait(W.at[0], c_s)
    wait(H, rc_s)
    wait(wait_f, f_s)


def body(nc, nx, nz, inputs, cotangent, doc_lengths, norm_gain, w_qkv, w_out):
    rows, width = inputs.shape[1:]
    layers, pairs, dps = 2 * nc, nc, nx * nz * 2
    local = SUB * dps
    grain = SUB * nc
    d = lax.axis_index("dp")
    gain = lax.dynamic_slice(norm_gain[0], (d * grain,), (grain,)).astype(F32)[:, None]
    wq = (w_qkv[0].astype(F32) * gain).astype(BF16)
    wg = jnp.concatenate([wq, w_out[0].T], axis=1)
    wg = jnp.stack([wg[:, :128], wg[:, 128:]])
    vmem = pl.BlockSpec(memory_space=pltpu.VMEM)
    anywhere = pl.BlockSpec(memory_space=pl.ANY)
    dma = pltpu.SemaphoreType.DMA
    xrows, zrows = 2 * SUB * nz, 2 * SUB
    sums = pl.pallas_call(
        functools.partial(kernel, nc, nx, nz, rows),
        out_shape=jax.ShapeDtypeStruct((2, grain, 128), F32),
        in_specs=[anywhere, anywhere, pl.BlockSpec(memory_space=pltpu.SMEM), vmem],
        out_specs=vmem,
        scratch_shapes=[
            pltpu.VMEM((2, layers, local, 128), BF16),
            pltpu.VMEM((rows, width), BF16),
            pltpu.VMEM((rows, width), BF16),
            pltpu.VMEM((layers, rows, local), BF16),
            pltpu.VMEM((layers, rows, local), BF16),
            pltpu.VMEM((layers, rows, 128), BF16),
            pltpu.VMEM((layers, rows, 128), BF16),
            pltpu.VMEM((layers, rows, 128), BF16),
            pltpu.VMEM((layers, rows, rows), F32),
            pltpu.VMEM((layers, rows, 128), BF16),
            pltpu.VMEM((layers, rows, 128), F32),
            pltpu.VMEM((layers, 2, rows, 128), BF16),
            pltpu.VMEM((pairs, 128, 384), BF16),
            pltpu.VMEM((pairs, rows, 128), F32),
            pltpu.VMEM((2, rows, 512), BF16),
            pltpu.VMEM((2, max(nc - 1, 1), rows, 512), BF16),
            pltpu.VMEM((2, rows, 128), BF16),
            pltpu.VMEM((2, max(nc - 1, 1), rows, 128), BF16),
            pltpu.VMEM((pairs, 64, 384), BF16),
            pltpu.VMEM((pairs, max(nc - 1, 1), 64, 384), BF16),
            pltpu.VMEM((2, layers, local, 128), BF16),
            pltpu.VMEM((layers, local, 128), BF16),
            pltpu.VMEM((layers, local, 128), BF16),
            pltpu.VMEM((pairs, max(nx - 1, 1), 2, xrows, 128), BF16),
            pltpu.VMEM((layers, xrows, 128), BF16),
            pltpu.VMEM((pairs, max(nz - 1, 1), 2, zrows, 128), BF16),
            pltpu.VMEM((2 * layers, SUB, 128), F32),
            pltpu.VMEM((2 * layers, SUB, 128), BF16),
            pltpu.VMEM((layers, zrows, 128), F32),
            pltpu.VMEM((2, 2, grain, 128), F32),
            dma((3,)),
            dma, dma,
            dma, dma((pairs,)), dma, dma((pairs,)), dma, dma((pairs,)),
            dma((2,)), dma((2,)), dma((2,)), dma((2,)), dma((pairs,)), dma((pairs,)),
            dma, dma((pairs,)), dma, dma((pairs,)), dma, dma((pairs,)),
            dma, dma,
        ],
        compiler_params=pltpu.CompilerParams(
            collective_id=0, has_side_effects=True, vmem_limit_bytes=60 * 2**20
        ),
        cost_estimate=pl.CostEstimate(
            flops=24 * layers * rows * local * 256,
            bytes_accessed=4 * rows * width,
            transcendentals=layers * rows * rows,
        ),
    )(inputs, cotangent, doc_lengths[:, 0, :], wg)
    full = jnp.concatenate([sums[0], sums[1]], axis=1)
    return ((full[:, :192] * gain)[None], full[:, 192:].T[None])


def solution(mesh, nx=4, nz=8):
    nc = mesh.shape["section"] // 2
    return jax.shard_map(
        functools.partial(body, nc, nx, nz),
        mesh=mesh,
        in_specs=(
            P(None, "dp", None),
            P(None, "dp", None),
            P(None, "dp", None),
            P("section", None),
            P("section", "dp", None),
            P("section", None, "dp"),
        ),
        out_specs=(P("section", "dp", None), P("section", None, "dp")),
        check_vma=False,
    )
```

```python
import functools

import jax
import jax.numpy as jnp
from jax import lax
from jax.experimental import pallas as pl
from jax.experimental.pallas import tpu as pltpu
from jax.sharding import PartitionSpec as P

MESH = pl.DeviceIdType.MESH
F32, BF16 = jnp.float32, jnp.bfloat16
SUB = 16


def nn(a, b):
    return jnp.dot(a, b, preferred_element_type=F32)


def nt(a, b):
    return lax.dot_general(a, b, (((1,), (1,)), ((), ())), preferred_element_type=F32)


def tn(a, b):
    return lax.dot_general(a, b, (((0,), (0,)), ((), ())), preferred_element_type=F32)


def kernel(
    nc, nx, nz, rows,
    inp, cot, lens, wg, out,
    W, xin, cin, X, DY, QK, KK, VV, PR, ATT, SC, SD, GM, UA,
    es, er, bs, br, gs, gr, G, SR, H, XR, H2, ZR, TALLY, TALLYB, FS, OB,
    in_sem, s1_s, s1_r, z_s, z_r, x_s, x_r, c_s, c_r,
    e_s, e_r, b_s, b_r, g_s, g_r, h_s, h_r, rc_s, rc_r, rx_s, rx_r, rz_s, rz_r, f_s, f_r,
):
    layers, pairs = 2 * nc, nc
    dps = nx * nz * 2
    local = SUB * dps
    width = local * nc
    zrows, xrows = 2 * SUB, 2 * SUB * nz
    s, d = lax.axis_index("section"), lax.axis_index("dp")
    c, k = lax.div(s, 2), lax.rem(s, 2)
    x, z, y = lax.div(d, 2 * nz), lax.rem(lax.div(d, 2), nz), lax.rem(d, 2)

    def at(start, size):
        return pl.ds(pl.multiple_of(start, SUB), size)

    def two(m):
        return pl.ds(2 * m, 2)

    def dp_of(px, pz, py):
        return (px * nz + pz) * 2 + py

    def far_first(n):
        return sorted(range(1, n), key=lambda o: -min(o, n - o))

    def column_peer(o):
        n = lax.rem(y * layers + s + o, 2 * layers)
        return lax.rem(n, layers), lax.div(n, layers)

    def chip_peer(o):
        return (2 * lax.rem(c + o, nc) + k, d)

    def x_peer(o):
        return lax.rem(x + o, nx)

    def z_peer(o):
        return lax.rem(z + o, nz)

    sibling = (2 * c + 1 - k, d)

    def send(src, dst, send_sem, recv_sem, device):
        pltpu.make_async_remote_copy(
            src_ref=src, dst_ref=dst, send_sem=send_sem, recv_sem=recv_sem,
            device_id=device, device_id_type=MESH,
        ).start()

    def wait(ref, sem):
        pltpu.make_async_copy(ref, ref, sem).wait()

    load_x = pltpu.make_async_copy(inp.at[k], xin, in_sem.at[0])
    load_c = pltpu.make_async_copy(cot.at[k], cin, in_sem.at[1])
    own = pltpu.make_async_copy(
        wg.at[k, at(SUB * c, SUB)], W.at[k, s, at(SUB * d, SUB)], in_sem.at[2]
    )
    load_x.start()
    load_c.start()
    own.start()

    barrier = pltpu.get_barrier_semaphore()
    peers = []
    for o in range(1, 2 * layers):
        t, ty = column_peer(o)
        peers += [(t, dp_of(x, z, ty))]
    peers += [(s, dp_of(x_peer(o), z, y)) for o in range(1, nx)]
    peers += [(s, dp_of(x, z_peer(o), y)) for o in range(1, nz)]
    for peer in peers:
        pl.semaphore_signal(barrier, inc=1, device_id=peer, device_id_type=MESH)
    grain = min(8, dps)
    big, small = grain * SUB * nc, grain * SUB
    at_row = lax.broadcasted_iota(jnp.int32, (big, small), 0)
    at_lane = lax.broadcasted_iota(jnp.int32, (big, small), 1)
    inside = at_lane & (SUB - 1)
    wanted = (at_lane - inside) * nc + inside + SUB * c
    pick = jnp.where(at_row == wanted, 1.0, 0.0).astype(BF16)

    def picked(source, m):
        return nn(source[:, m * big : (m + 1) * big], pick).astype(BF16)

    load_x.wait()
    for m in range(dps // grain):
        X[0, :, m * small : (m + 1) * small] = picked(xin, m)

    pl.semaphore_wait(barrier, len(peers))

    for o in range(1, 2 * layers):
        t, ty = column_peer(o)
        tc, tk = lax.div(t, 2), lax.rem(t, 2)
        send(
            wg.at[tk, at(SUB * tc, SUB)], W.at[tk, s, at(SUB * d, SUB)],
            s1_s, s1_r, (t, dp_of(x, z, ty)),
        )

    own.wait()
    columns = TALLYB.at[pl.ds(0, 2 * layers - 1)]
    wait(columns, s1_r)

    def z_gather(m):
        block = W.at[k, two(m), at(zrows * (x * nz + z), zrows)]
        for o in far_first(nz):
            send(block, block, z_s, z_r.at[m], (s, dp_of(x, z_peer(o), y)))

    def z_arrived(m):
        if nz > 1:
            wait(W.at[0, pl.ds(0, 2), pl.ds(0, zrows * (nz - 1))], z_r.at[m])

    def x_gather(m):
        block = W.at[k, two(m), at(xrows * x, xrows)]
        for o in far_first(nx):
            send(block, block, x_s, x_r.at[m], (s, dp_of(x_peer(o), z, y)))

    def x_arrived(m):
        if nx > 1:
            wait(W.at[0, pl.ds(0, 2), pl.ds(0, xrows * (nx - 1))], x_r.at[m])

    def core_gather(m):
        block = W.at[k, two(m)]
        send(block, block, c_s, c_r.at[m], sibling)

    half = at(32 * k, 32)

    def gamma(m):
        @pl.when(m > 0)
        def _():
            wait(W.at[0, pl.ds(0, 2)], c_r.at[m])

        a, b = 2 * m, 2 * m + 1
        right = jnp.concatenate([W[0, b], W[1, b], W[1, a]], axis=1)
        part = tn(W[1, a], right)[64:]
        gs[m] = part.astype(BF16)
        for o in far_first(nc):
            send(gs.at[m, half], gr.at[m, o - 1], g_s.at[m], g_r.at[m], chip_peer(o))

    def gamma_sum(m):
        total = gs[m, half].astype(F32)
        if nc > 1:
            wait(gr.at[m], g_r.at[m])
            for o in range(nc - 1):
                total = total + gr[m, o].astype(F32)
            wait(gr.at[m], g_s.at[m])
        GM[m, :64] = jnp.zeros((64, 384), BF16)
        mine = GM.at[m, at(64 + 32 * k, 32)]
        mine[...] = total.astype(BF16)
        send(mine, mine, h_s.at[m], h_r.at[m], sibling)

    def gamma_arrived(m):
        wait(GM.at[m, pl.ds(64, 32)], h_r.at[m])
        wait(GM.at[m, pl.ds(64, 32)], h_s.at[m])

    row = lax.broadcasted_iota(jnp.int32, (rows, rows), 0)
    col = lax.broadcasted_iota(jnp.int32, (rows, rows), 1)
    first = lens[k, 0]
    allowed = ((row < first) == (col < first)) & (row >= col)
    lane = lax.broadcasted_iota(jnp.int32, (rows, 128), 1)
    low = lane < 64

    def both(l):
        return jnp.concatenate([W[0, l], W[1, l]], axis=1)

    def attend(l, t0, t1, square):
        scale = lax.rsqrt(square * (1.0 / width) + 1e-05)
        q = t0 * scale
        kk = pltpu.roll(q, 64, 1).astype(BF16)
        vv = pltpu.roll(jnp.where(low, t1 * scale, 0.0), 64, 1).astype(BF16)
        scores = nt(jnp.where(low, q, 0.0).astype(BF16), kk) * 0.125
        scores = jnp.where(allowed, scores, -1e30)
        top = jnp.max(scores, axis=1, keepdims=True)
        e = jnp.exp(scores - top)
        p = e / jnp.sum(e, axis=1, keepdims=True)
        att = nn(p.astype(BF16), vv).astype(BF16)
        QK[l] = q.astype(BF16)
        KK[l] = kk
        VV[l] = vv
        PR[l] = p
        ATT[l] = att
        SC[l] = jnp.broadcast_to(scale, (rows, 128))
        return att

    def forward(m):
        slot = lax.rem(m, 2)
        a, b = 2 * m, 2 * m + 1
        xb = X[a]
        part = nn(xb, jnp.concatenate([both(a), both(b)], axis=1))
        wide = xb.astype(F32)
        square = jnp.sum(wide * wide, axis=1, keepdims=True)
        upper = square.astype(BF16).astype(F32)
        es[slot, :, :384] = part[:, :384].astype(BF16)
        tail = jnp.where(lane < 96, upper, square - upper)
        es[slot, :, 384:] = jnp.where(low, part[:, 384:], tail).astype(BF16)
        for o in far_first(nc):
            send(es.at[slot], er.at[slot, o - 1], e_s.at[slot], e_r.at[slot], chip_peer(o))
        between(m)
        gamma_sum(m)
        t = [part[:, 128 * i : 128 * (i + 1)] for i in range(4)]
        if nc > 1:
            wait(er.at[slot], e_r.at[slot])
            for o in range(nc - 1):
                for i in range(4):
                    t[i] = t[i] + er[slot, o, :, 128 * i : 128 * (i + 1)].astype(F32)
                more = er[slot, o, :, 384:].astype(F32)
                square = square + more[:, 64:65] + more[:, 96:97]
            wait(er.at[slot], e_s.at[slot])
        att = attend(a, t[0], t[1], square)
        gamma_arrived(m)
        u = nn(att, GM[m])
        into = jnp.where(low, 0.0, t[1])
        after = into + jnp.where(low, 0.0, u[:, 256:])
        UA[m] = after
        square = square + jnp.sum(att.astype(F32) * (into + after), axis=1, keepdims=True)
        last = attend(b, t[2] + u[:, :128], t[3] + u[:, 128:256], square)
        middle = (X[a].astype(F32) + nt(att, W[1, a])).astype(BF16)
        X[b] = middle

        @pl.when(m < pairs - 1)
        def _():
            X[b + 1] = (middle.astype(F32) + nt(last, W[1, b])).astype(BF16)

    def between(m):
        @pl.when(m == 0)
        def _():
            gamma(0)

        @pl.when(m + 2 < pairs)
        def _():
            z_arrived(m + 2)
            x_gather(m + 2)

        @pl.when(m + 3 < pairs)
        def _():
            z_gather(m + 3)

        @pl.when(m + 1 < pairs)
        def _():
            x_arrived(m + 1)
            core_gather(m + 1)
            gamma(m + 1)

    z_gather(0)
    load_c.wait()
    for m in range(dps // grain):
        DY[layers - 1, :, m * small : (m + 1) * small] = picked(cin, m)
    z_arrived(0)
    x_gather(0)
    if pairs > 1:
        z_gather(1)
        z_arrived(1)
        x_gather(1)
    if pairs > 2:
        z_gather(2)
    x_arrived(0)
    core_gather(0)
    wait(W.at[0, pl.ds(0, 2)], c_r.at[0])

    def forward_step(m, carry):
        forward(m)
        return carry

    lax.fori_loop(0, pairs, forward_step, 0)

    def grads(m):
        for l in (2 * m, 2 * m + 1):
            left = jnp.concatenate([X[l], DY[l]], axis=0)
            att = ATT[l]
            right = jnp.concatenate(
                [
                    jnp.concatenate([SD[l, 0], SD[l, 1]], axis=1),
                    jnp.concatenate([jnp.zeros_like(att), att], axis=1),
                ],
                axis=0,
            )
            g = tn(left, right)
            G[0, l] = g[:, :128].astype(BF16)
            G[1, l] = g[:, 128:].astype(BF16)
            send(G.at[1 - k, l], SR.at[l], rc_s, rc_r.at[m], sibling)

    def x_scatter(m):
        wait(SR.at[two(m)], rc_r.at[m])
        for i in range(2):
            l = 2 * m + i
            H[l] = (G[k, l].astype(F32) + SR[l].astype(F32)).astype(BF16)
            for o in far_first(nx):
                px = x_peer(o)
                send(
                    H.at[l, at(xrows * px, xrows)], XR.at[m, o - 1, i],
                    rx_s, rx_r.at[m], (s, dp_of(px, z, y)),
                )

    def z_scatter(m):
        total = H[two(m), at(xrows * x, xrows)].astype(F32)
        if nx > 1:
            wait(XR.at[m], rx_r.at[m])
            for o in range(nx - 1):
                total = total + XR[m, o].astype(F32)
        H2[two(m)] = total.astype(BF16)
        for o in far_first(nz):
            pz = z_peer(o)
            send(
                H2.at[two(m), at(zrows * pz, zrows)], ZR.at[m, o - 1],
                rz_s, rz_r.at[m], (s, dp_of(x, pz, y)),
            )

    def finish(m):
        total = H2[two(m), at(zrows * z, zrows)].astype(F32)
        if nz > 1:
            wait(ZR.at[m], rz_r.at[m])
            for o in range(nz - 1):
                total = total + ZR[m, o].astype(F32)
        FS[two(m)] = total

    def staged(m, behind, stage):
        @pl.when((m + behind >= 0) & (m + behind < pairs))
        def _():
            stage(m + behind)

    def attend_back(l, da):
        da = jnp.where(low, 0.0, da).astype(BF16)
        vv, kk, p, scale = VV[l], KK[l], PR[l], SC[l]
        dp = nt(da, vv)
        ds = p * (dp - jnp.sum(p * dp, axis=1, keepdims=True)) * 0.125
        ds = ds.astype(BF16)
        dqk = jnp.where(low, nn(ds, kk), tn(ds, kk))
        dv = tn(p.astype(BF16), da)
        dot = dqk * QK[l].astype(F32) + dv * vv.astype(F32)
        dot = jnp.sum(dot, axis=1, keepdims=True)
        coef = scale[:, :1] * scale[:, :1] * dot * (1.0 / width)
        sd0 = (dqk * scale).astype(BF16)
        sd1 = (pltpu.roll(dv, 64, 1) * scale).astype(BF16)
        SD[l, 0] = sd0
        SD[l, 1] = sd1
        return jnp.concatenate([sd0, sd1], axis=1), coef

    def down(l, sd, coef):
        change = nt(sd, both(l)) - X[l].astype(F32) * coef
        DY[l - 1] = (DY[l].astype(F32) + change).astype(BF16)

    def backward_step(step, carry):
        m = pairs - 1 - step
        slot = lax.rem(step, 2)
        a, b = 2 * m, 2 * m + 1

        @pl.when(m >= 0)
        def _():
            part = nn(DY[b], jnp.concatenate([W[1, b], W[1, a]], axis=1))
            part = jnp.where(low, pltpu.roll(part[:, 128:], 64, 1), part[:, :128])
            bs[slot] = part.astype(BF16)
            for o in far_first(nc):
                send(bs.at[slot], br.at[slot, o - 1], b_s.at[slot], b_r.at[slot], chip_peer(o))

        staged(m, 1, grads)
        staged(m, 3, finish)
        staged(m, 1, x_scatter)
        staged(m, 2, z_scatter)

        @pl.when(m >= 0)
        def _():
            total = bs[slot].astype(F32)
            if nc > 1:
                wait(br.at[slot], b_r.at[slot])
                for o in range(nc - 1):
                    total = total + br[slot, o].astype(F32)
                wait(br.at[slot], b_s.at[slot])
            sd, coef = attend_back(b, total)
            other = nt(sd, GM[m, :, :256]) - UA[m] * coef
            down(b, sd, coef)
            sd, coef = attend_back(a, pltpu.roll(total, 64, 1) + other)

            @pl.when(m > 0)
            def _():
                down(a, sd, coef)

        return carry

    lax.fori_loop(0, pairs + 3, backward_step, 0)

    for o in range(1, 2 * layers):
        t, ty = column_peer(o)
        send(
            FS.at[t, at(SUB * ty, SUB)], OB.at[y, k, at(SUB * c, SUB)],
            f_s, f_r, (t, dp_of(x, z, ty)),
        )
    OB[y, k, at(SUB * c, SUB)] = FS[s, at(SUB * y, SUB)]
    wait_f = TALLY.at[pl.ds(0, 2 * layers - 1)]
    wait(wait_f, f_r)
    out[...] = OB[0] + OB[1]

    wait(columns, s1_s)
    if nz > 1:
        for o in range(1, nz):
            wait(W.at[0, :, pl.ds(0, zrows)], z_s)
            wait(H2.at[:, pl.ds(0, zrows)], rz_s)
    if nx > 1:
        for o in range(1, nx):
            wait(W.at[0, :, pl.ds(0, xrows)], x_s)
            wait(H2, rx_s)
    wait(W.at[0], c_s)
    wait(H, rc_s)
    wait(wait_f, f_s)


def body(nc, nx, nz, inputs, cotangent, doc_lengths, norm_gain, w_qkv, w_out):
    rows, width = inputs.shape[1:]
    layers, pairs, dps = 2 * nc, nc, nx * nz * 2
    local = SUB * dps
    grain = SUB * nc
    d = lax.axis_index("dp")
    gain = lax.dynamic_slice(norm_gain[0], (d * grain,), (grain,)).astype(F32)[:, None]
    wq = (w_qkv[0].astype(F32) * gain).astype(BF16)
    wg = jnp.concatenate([wq, w_out[0].T], axis=1)
    wg = jnp.stack([wg[:, :128], wg[:, 128:]])
    vmem = pl.BlockSpec(memory_space=pltpu.VMEM)
    anywhere = pl.BlockSpec(memory_space=pl.ANY)
    dma = pltpu.SemaphoreType.DMA
    xrows, zrows = 2 * SUB * nz, 2 * SUB
    sums = pl.pallas_call(
        functools.partial(kernel, nc, nx, nz, rows),
        out_shape=jax.ShapeDtypeStruct((2, grain, 128), F32),
        in_specs=[anywhere, anywhere, pl.BlockSpec(memory_space=pltpu.SMEM), vmem],
        out_specs=vmem,
        scratch_shapes=[
            pltpu.VMEM((2, layers, local, 128), BF16),
            pltpu.VMEM((rows, width), BF16),
            pltpu.VMEM((rows, width), BF16),
            pltpu.VMEM((layers, rows, local), BF16),
            pltpu.VMEM((layers, rows, local), BF16),
            pltpu.VMEM((layers, rows, 128), BF16),
            pltpu.VMEM((layers, rows, 128), BF16),
            pltpu.VMEM((layers, rows, 128), BF16),
            pltpu.VMEM((layers, rows, rows), F32),
            pltpu.VMEM((layers, rows, 128), BF16),
            pltpu.VMEM((layers, rows, 128), F32),
            pltpu.VMEM((layers, 2, rows, 128), BF16),
            pltpu.VMEM((pairs, 128, 384), BF16),
            pltpu.VMEM((pairs, rows, 128), F32),
            pltpu.VMEM((2, rows, 512), BF16),
            pltpu.VMEM((2, max(nc - 1, 1), rows, 512), BF16),
            pltpu.VMEM((2, rows, 128), BF16),
            pltpu.VMEM((2, max(nc - 1, 1), rows, 128), BF16),
            pltpu.VMEM((pairs, 64, 384), BF16),
            pltpu.VMEM((pairs, max(nc - 1, 1), 32, 384), BF16),
            pltpu.VMEM((2, layers, local, 128), BF16),
            pltpu.VMEM((layers, local, 128), BF16),
            pltpu.VMEM((layers, local, 128), BF16),
            pltpu.VMEM((pairs, max(nx - 1, 1), 2, xrows, 128), BF16),
            pltpu.VMEM((layers, xrows, 128), BF16),
            pltpu.VMEM((pairs, max(nz - 1, 1), 2, zrows, 128), BF16),
            pltpu.VMEM((2 * layers, SUB, 128), F32),
            pltpu.VMEM((2 * layers, SUB, 128), BF16),
            pltpu.VMEM((layers, zrows, 128), F32),
            pltpu.VMEM((2, 2, grain, 128), F32),
            dma((3,)),
            dma, dma,
            dma, dma((pairs,)), dma, dma((pairs,)), dma, dma((pairs,)),
            dma((2,)), dma((2,)), dma((2,)), dma((2,)), dma((pairs,)), dma((pairs,)),
            dma((pairs,)), dma((pairs,)),
            dma, dma((pairs,)), dma, dma((pairs,)), dma, dma((pairs,)),
            dma, dma,
        ],
        compiler_params=pltpu.CompilerParams(
            collective_id=0, has_side_effects=True, vmem_limit_bytes=60 * 2**20
        ),
        cost_estimate=pl.CostEstimate(
            flops=24 * layers * rows * local * 256,
            bytes_accessed=4 * rows * width,
            transcendentals=layers * rows * rows,
        ),
    )(inputs, cotangent, doc_lengths[:, 0, :], wg)
    full = jnp.concatenate([sums[0], sums[1]], axis=1)
    return ((full[:, :192] * gain)[None], full[:, 192:].T[None])


def solution(mesh, nx=4, nz=8):
    nc = mesh.shape["section"] // 2
    return jax.shard_map(
        functools.partial(body, nc, nx, nz),
        mesh=mesh,
        in_specs=(
            P(None, "dp", None),
            P(None, "dp", None),
            P(None, "dp", None),
            P("section", None),
            P("section", "dp", None),
            P("section", None, "dp"),
        ),
        out_specs=(P("section", "dp", None), P("section", None, "dp")),
        check_vma=False,
    )
```

```python
import functools

import jax
import jax.numpy as jnp
from jax import lax
from jax.experimental import pallas as pl
from jax.experimental.pallas import tpu as pltpu
from jax.sharding import PartitionSpec as P

MESH = pl.DeviceIdType.MESH
F32, BF16 = jnp.float32, jnp.bfloat16
SUB = 16


def nn(a, b):
    return jnp.dot(a, b, preferred_element_type=F32)


def nt(a, b):
    return lax.dot_general(a, b, (((1,), (1,)), ((), ())), preferred_element_type=F32)


def tn(a, b):
    return lax.dot_general(a, b, (((0,), (0,)), ((), ())), preferred_element_type=F32)


def kernel(
    nc, nx, nz, rows,
    inp, cot, lens, wg, out,
    W, xin, cin, X, DY, QK, KK, VV, PR, ATT, SC, SD, GM, UA,
    es, er, bs, br, gs, gr, G, SR, H, XR, H2, ZR, TALLY, TALLYB, FS, OB,
    in_sem, s1_s, s1_r, z_s, z_r, x_s, x_r, c_s, c_r,
    e_s, e_r, b_s, b_r, g_s, g_r, h_s, h_r, rc_s, rc_r, rx_s, rx_r, rz_s, rz_r, f_s, f_r,
):
    layers, pairs = 2 * nc, nc
    dps = nx * nz * 2
    local = SUB * dps
    width = local * nc
    zrows, xrows = 2 * SUB, 2 * SUB * nz
    s, d = lax.axis_index("section"), lax.axis_index("dp")
    c, k = lax.div(s, 2), lax.rem(s, 2)
    x, z, y = lax.div(d, 2 * nz), lax.rem(lax.div(d, 2), nz), lax.rem(d, 2)

    def at(start, size):
        return pl.ds(pl.multiple_of(start, SUB), size)

    def two(m):
        return pl.ds(2 * m, 2)

    def dp_of(px, pz, py):
        return (px * nz + pz) * 2 + py

    def far_first(n):
        return sorted(range(1, n), key=lambda o: -min(o, n - o))

    def column_peer(o):
        n = lax.rem(y * layers + s + o, 2 * layers)
        return lax.rem(n, layers), lax.div(n, layers)

    def chip_peer(o):
        return (2 * lax.rem(c + o, nc) + k, d)

    def x_peer(o):
        return lax.rem(x + o, nx)

    def z_peer(o):
        return lax.rem(z + o, nz)

    sibling = (2 * c + 1 - k, d)

    def send(src, dst, send_sem, recv_sem, device):
        pltpu.make_async_remote_copy(
            src_ref=src, dst_ref=dst, send_sem=send_sem, recv_sem=recv_sem,
            device_id=device, device_id_type=MESH,
        ).start()

    def wait(ref, sem):
        pltpu.make_async_copy(ref, ref, sem).wait()

    load_x = pltpu.make_async_copy(inp.at[k], xin, in_sem.at[0])
    load_c = pltpu.make_async_copy(cot.at[k], cin, in_sem.at[1])
    own = pltpu.make_async_copy(
        wg.at[k, at(SUB * c, SUB)], W.at[k, s, at(SUB * d, SUB)], in_sem.at[2]
    )
    load_x.start()
    load_c.start()
    own.start()

    barrier = pltpu.get_barrier_semaphore()
    peers = []
    for o in range(1, 2 * layers):
        t, ty = column_peer(o)
        peers += [(t, dp_of(x, z, ty))]
    peers += [(s, dp_of(x_peer(o), z, y)) for o in range(1, nx)]
    peers += [(s, dp_of(x, z_peer(o), y)) for o in range(1, nz)]
    for peer in peers:
        pl.semaphore_signal(barrier, inc=1, device_id=peer, device_id_type=MESH)
    grain = min(8, dps)
    big, small = grain * SUB * nc, grain * SUB
    at_row = lax.broadcasted_iota(jnp.int32, (big, small), 0)
    at_lane = lax.broadcasted_iota(jnp.int32, (big, small), 1)
    inside = at_lane & (SUB - 1)
    wanted = (at_lane - inside) * nc + inside + SUB * c
    pick = jnp.where(at_row == wanted, 1.0, 0.0).astype(BF16)

    def picked(source, m):
        return nn(source[:, m * big : (m + 1) * big], pick).astype(BF16)

    load_x.wait()
    for m in range(dps // grain):
        X[0, :, m * small : (m + 1) * small] = picked(xin, m)

    pl.semaphore_wait(barrier, len(peers))

    for o in range(1, 2 * layers):
        t, ty = column_peer(o)
        tc, tk = lax.div(t, 2), lax.rem(t, 2)
        send(
            wg.at[tk, at(SUB * tc, SUB)], W.at[tk, s, at(SUB * d, SUB)],
            s1_s, s1_r, (t, dp_of(x, z, ty)),
        )

    own.wait()
    columns = TALLYB.at[pl.ds(0, 2 * layers - 1)]
    wait(columns, s1_r)

    def z_gather(m):
        block = W.at[k, two(m), at(zrows * (x * nz + z), zrows)]
        for o in far_first(nz):
            send(block, block, z_s, z_r.at[m], (s, dp_of(x, z_peer(o), y)))

    def z_arrived(m):
        if nz > 1:
            wait(W.at[0, pl.ds(0, 2), pl.ds(0, zrows * (nz - 1))], z_r.at[m])

    def x_gather(m):
        block = W.at[k, two(m), at(xrows * x, xrows)]
        for o in far_first(nx):
            send(block, block, x_s, x_r.at[m], (s, dp_of(x_peer(o), z, y)))

    def x_arrived(m):
        if nx > 1:
            wait(W.at[0, pl.ds(0, 2), pl.ds(0, xrows * (nx - 1))], x_r.at[m])

    def core_gather(m):
        block = W.at[k, two(m)]
        send(block, block, c_s, c_r.at[m], sibling)

    half = at(32 * k, 32)

    def gamma(m):
        @pl.when(m > 0)
        def _():
            wait(W.at[0, pl.ds(0, 2)], c_r.at[m])

        a, b = 2 * m, 2 * m + 1
        right = jnp.concatenate([W[0, b], W[1, b], W[1, a]], axis=1)
        part = tn(W[1, a], right)[64:]
        gs[m] = part.astype(BF16)
        for o in far_first(nc):
            send(gs.at[m, half], gr.at[m, o - 1], g_s.at[m], g_r.at[m], chip_peer(o))

    def gamma_sum(m):
        total = gs[m, half].astype(F32)
        if nc > 1:
            wait(gr.at[m], g_r.at[m])
            for o in range(nc - 1):
                total = total + gr[m, o].astype(F32)
            wait(gr.at[m], g_s.at[m])
        GM[m, :64] = jnp.zeros((64, 384), BF16)
        mine = GM.at[m, at(64 + 32 * k, 32)]
        mine[...] = total.astype(BF16)
        send(mine, mine, h_s.at[m], h_r.at[m], sibling)

    def gamma_arrived(m):
        wait(GM.at[m, pl.ds(64, 32)], h_r.at[m])
        wait(GM.at[m, pl.ds(64, 32)], h_s.at[m])

    row = lax.broadcasted_iota(jnp.int32, (rows, rows), 0)
    col = lax.broadcasted_iota(jnp.int32, (rows, rows), 1)
    first = lens[k, 0]
    allowed = ((row < first) == (col < first)) & (row >= col)
    lane = lax.broadcasted_iota(jnp.int32, (rows, 128), 1)
    low = lane < 64

    def both(l):
        return jnp.concatenate([W[0, l], W[1, l]], axis=1)

    def attend(l, t0, t1, square):
        scale = lax.rsqrt(square * (1.0 / width) + 1e-05)
        q = t0 * scale
        kk = pltpu.roll(q, 64, 1).astype(BF16)
        vv = pltpu.roll(jnp.where(low, t1 * scale, 0.0), 64, 1).astype(BF16)
        scores = nt(jnp.where(low, q, 0.0).astype(BF16), kk) * 0.125
        scores = jnp.where(allowed, scores, -1e30)
        top = jnp.max(scores, axis=1, keepdims=True)
        e = jnp.exp(scores - top)
        p = e / jnp.sum(e, axis=1, keepdims=True)
        att = nn(p.astype(BF16), vv).astype(BF16)
        QK[l] = q.astype(BF16)
        KK[l] = kk
        VV[l] = vv
        PR[l] = p
        ATT[l] = att
        SC[l] = jnp.broadcast_to(scale, (rows, 128))
        return att

    def forward(m):
        slot = lax.rem(m, 2)
        a, b = 2 * m, 2 * m + 1
        xb = X[a]
        part = nn(xb, jnp.concatenate([both(a), both(b)], axis=1))
        wide = xb.astype(F32)
        square = jnp.sum(wide * wide, axis=1, keepdims=True)
        upper = square.astype(BF16).astype(F32)
        es[slot, :, :384] = part[:, :384].astype(BF16)
        tail = jnp.where(lane < 96, upper, square - upper)
        es[slot, :, 384:] = jnp.where(low, part[:, 384:], tail).astype(BF16)
        for o in far_first(nc):
            send(es.at[slot], er.at[slot, o - 1], e_s.at[slot], e_r.at[slot], chip_peer(o))
        between(m)
        gamma_sum(m)
        t = [part[:, 128 * i : 128 * (i + 1)] for i in range(4)]
        if nc > 1:
            wait(er.at[slot], e_r.at[slot])
            for o in range(nc - 1):
                for i in range(4):
                    t[i] = t[i] + er[slot, o, :, 128 * i : 128 * (i + 1)].astype(F32)
                more = er[slot, o, :, 384:].astype(F32)
                square = square + more[:, 64:65] + more[:, 96:97]
            wait(er.at[slot], e_s.at[slot])
        att = attend(a, t[0], t[1], square)
        gamma_arrived(m)
        u = nn(att, GM[m])
        into = jnp.where(low, 0.0, t[1])
        after = into + jnp.where(low, 0.0, u[:, 256:])
        UA[m] = after
        square = square + jnp.sum(att.astype(F32) * (into + after), axis=1, keepdims=True)
        last = attend(b, t[2] + u[:, :128], t[3] + u[:, 128:256], square)
        middle = (X[a].astype(F32) + nt(att, W[1, a])).astype(BF16)
        X[b] = middle

        @pl.when(m < pairs - 1)
        def _():
            X[b + 1] = (middle.astype(F32) + nt(last, W[1, b])).astype(BF16)

    def between(m):
        @pl.when(m == 0)
        def _():
            gamma(0)

        @pl.when(m + 2 < pairs)
        def _():
            z_arrived(m + 2)
            x_gather(m + 2)

        @pl.when(m + 3 < pairs)
        def _():
            z_gather(m + 3)

        @pl.when(m + 1 < pairs)
        def _():
            x_arrived(m + 1)
            core_gather(m + 1)
            gamma(m + 1)

    z_gather(0)
    load_c.wait()
    for m in range(dps // grain):
        DY[layers - 1, :, m * small : (m + 1) * small] = picked(cin, m)
    z_arrived(0)
    x_gather(0)
    if pairs > 1:
        z_gather(1)
        z_arrived(1)
        x_gather(1)
    if pairs > 2:
        z_gather(2)
    x_arrived(0)
    core_gather(0)
    wait(W.at[0, pl.ds(0, 2)], c_r.at[0])

    def forward_step(m, carry):
        forward(m)
        return carry

    lax.fori_loop(0, pairs, forward_step, 0)

    def grads_of(l):
        left = jnp.concatenate([X[l], DY[l]], axis=0)
        att = ATT[l]
        right = jnp.concatenate(
            [
                jnp.concatenate([SD[l, 0], SD[l, 1]], axis=1),
                jnp.concatenate([jnp.zeros_like(att), att], axis=1),
            ],
            axis=0,
        )
        g = tn(left, right)
        G[0, l] = g[:, :128].astype(BF16)
        G[1, l] = g[:, 128:].astype(BF16)
        send(G.at[1 - k, l], SR.at[l], rc_s, rc_r.at[l], sibling)

    def scatter_of(m, i):
        l = 2 * m + i
        wait(SR.at[l], rc_r.at[l])
        H[l] = (G[k, l].astype(F32) + SR[l].astype(F32)).astype(BF16)
        for o in far_first(nx):
            px = x_peer(o)
            send(
                H.at[l, at(xrows * px, xrows)], XR.at[m, o - 1, i],
                rx_s, rx_r.at[m], (s, dp_of(px, z, y)),
            )

    def grads(m):
        @pl.when(m > 0)
        def _():
            grads_of(2 * m + 1)

        grads_of(2 * m)

    def x_scatter(m):
        @pl.when(m > 0)
        def _():
            scatter_of(m, 1)

        scatter_of(m, 0)

    def z_scatter(m):
        total = H[two(m), at(xrows * x, xrows)].astype(F32)
        if nx > 1:
            wait(XR.at[m], rx_r.at[m])
            for o in range(nx - 1):
                total = total + XR[m, o].astype(F32)
        H2[two(m)] = total.astype(BF16)
        for o in far_first(nz):
            pz = z_peer(o)
            send(
                H2.at[two(m), at(zrows * pz, zrows)], ZR.at[m, o - 1],
                rz_s, rz_r.at[m], (s, dp_of(x, pz, y)),
            )

    def finish(m):
        total = H2[two(m), at(zrows * z, zrows)].astype(F32)
        if nz > 1:
            wait(ZR.at[m], rz_r.at[m])
            for o in range(nz - 1):
                total = total + ZR[m, o].astype(F32)
        FS[two(m)] = total
        for i in range(2):
            for ty in range(2):
                to_holder(2 * m + i, ty)

    def to_holder(l, ty):
        here = (l == s) & (y == ty)
        sums = FS.at[l, pl.ds(SUB * ty, SUB)]
        place = OB.at[y, k, at(SUB * c, SUB)]

        @pl.when(here)
        def _():
            place[...] = sums[...]

        @pl.when(jnp.logical_not(here))
        def _():
            send(sums, place, f_s, f_r, (l, dp_of(x, z, ty)))

    def staged(m, behind, stage):
        @pl.when((m + behind >= 0) & (m + behind < pairs))
        def _():
            stage(m + behind)

    def attend_back(l, da):
        da = jnp.where(low, 0.0, da).astype(BF16)
        vv, kk, p, scale = VV[l], KK[l], PR[l], SC[l]
        dp = nt(da, vv)
        ds = p * (dp - jnp.sum(p * dp, axis=1, keepdims=True)) * 0.125
        ds = ds.astype(BF16)
        dqk = jnp.where(low, nn(ds, kk), tn(ds, kk))
        dv = tn(p.astype(BF16), da)
        dot = dqk * QK[l].astype(F32) + dv * vv.astype(F32)
        dot = jnp.sum(dot, axis=1, keepdims=True)
        coef = scale[:, :1] * scale[:, :1] * dot * (1.0 / width)
        sd0 = (dqk * scale).astype(BF16)
        sd1 = (pltpu.roll(dv, 64, 1) * scale).astype(BF16)
        SD[l, 0] = sd0
        SD[l, 1] = sd1
        return jnp.concatenate([sd0, sd1], axis=1), coef

    def down(l, sd, coef):
        change = nt(sd, both(l)) - X[l].astype(F32) * coef
        DY[l - 1] = (DY[l].astype(F32) + change).astype(BF16)

    def backward_step(step, carry):
        m = pairs - 1 - step
        slot = lax.rem(step, 2)
        a, b = 2 * m, 2 * m + 1

        @pl.when(m >= 0)
        def _():
            part = nn(DY[b], jnp.concatenate([W[1, b], W[1, a]], axis=1))
            part = jnp.where(low, pltpu.roll(part[:, 128:], 64, 1), part[:, :128])
            bs[slot] = part.astype(BF16)
            for o in far_first(nc):
                send(bs.at[slot], br.at[slot, o - 1], b_s.at[slot], b_r.at[slot], chip_peer(o))

        staged(m, 1, grads)
        staged(m, 3, finish)
        staged(m, 1, x_scatter)
        staged(m, 2, z_scatter)

        @pl.when(m >= 0)
        def _():
            total = bs[slot].astype(F32)
            if nc > 1:
                wait(br.at[slot], b_r.at[slot])
                for o in range(nc - 1):
                    total = total + br[slot, o].astype(F32)
                wait(br.at[slot], b_s.at[slot])
            sd, coef = attend_back(b, total)
            other = nt(sd, GM[m, :, :256]) - UA[m] * coef
            down(b, sd, coef)

            @pl.when(m == 0)
            def _():
                grads_of(b)

            sd, coef = attend_back(a, pltpu.roll(total, 64, 1) + other)

            @pl.when(m == 0)
            def _():
                scatter_of(m, 1)

            @pl.when(m > 0)
            def _():
                down(a, sd, coef)

        return carry

    lax.fori_loop(0, pairs + 3, backward_step, 0)

    wait_f = TALLY.at[pl.ds(0, 2 * layers - 1)]
    wait(wait_f, f_r)
    out[...] = OB[0] + OB[1]

    wait(columns, s1_s)
    if nz > 1:
        for o in range(1, nz):
            wait(W.at[0, :, pl.ds(0, zrows)], z_s)
            wait(H2.at[:, pl.ds(0, zrows)], rz_s)
    if nx > 1:
        for o in range(1, nx):
            wait(W.at[0, :, pl.ds(0, xrows)], x_s)
            wait(H2, rx_s)
    wait(W.at[0], c_s)
    wait(H, rc_s)
    wait(wait_f, f_s)


def body(nc, nx, nz, inputs, cotangent, doc_lengths, norm_gain, w_qkv, w_out):
    rows, width = inputs.shape[1:]
    layers, pairs, dps = 2 * nc, nc, nx * nz * 2
    local = SUB * dps
    grain = SUB * nc
    d = lax.axis_index("dp")
    gain = lax.dynamic_slice(norm_gain[0], (d * grain,), (grain,)).astype(F32)[:, None]
    wq = (w_qkv[0].astype(F32) * gain).astype(BF16)
    wg = jnp.concatenate([wq, w_out[0].T], axis=1)
    wg = jnp.stack([wg[:, :128], wg[:, 128:]])
    vmem = pl.BlockSpec(memory_space=pltpu.VMEM)
    anywhere = pl.BlockSpec(memory_space=pl.ANY)
    dma = pltpu.SemaphoreType.DMA
    xrows, zrows = 2 * SUB * nz, 2 * SUB
    sums = pl.pallas_call(
        functools.partial(kernel, nc, nx, nz, rows),
        out_shape=jax.ShapeDtypeStruct((2, grain, 128), F32),
        in_specs=[anywhere, anywhere, pl.BlockSpec(memory_space=pltpu.SMEM), vmem],
        out_specs=vmem,
        scratch_shapes=[
            pltpu.VMEM((2, layers, local, 128), BF16),
            pltpu.VMEM((rows, width), BF16),
            pltpu.VMEM((rows, width), BF16),
            pltpu.VMEM((layers, rows, local), BF16),
            pltpu.VMEM((layers, rows, local), BF16),
            pltpu.VMEM((layers, rows, 128), BF16),
            pltpu.VMEM((layers, rows, 128), BF16),
            pltpu.VMEM((layers, rows, 128), BF16),
            pltpu.VMEM((layers, rows, rows), F32),
            pltpu.VMEM((layers, rows, 128), BF16),
            pltpu.VMEM((layers, rows, 128), F32),
            pltpu.VMEM((layers, 2, rows, 128), BF16),
            pltpu.VMEM((pairs, 128, 384), BF16),
            pltpu.VMEM((pairs, rows, 128), F32),
            pltpu.VMEM((2, rows, 512), BF16),
            pltpu.VMEM((2, max(nc - 1, 1), rows, 512), BF16),
            pltpu.VMEM((2, rows, 128), BF16),
            pltpu.VMEM((2, max(nc - 1, 1), rows, 128), BF16),
            pltpu.VMEM((pairs, 64, 384), BF16),
            pltpu.VMEM((pairs, max(nc - 1, 1), 32, 384), BF16),
            pltpu.VMEM((2, layers, local, 128), BF16),
            pltpu.VMEM((layers, local, 128), BF16),
            pltpu.VMEM((layers, local, 128), BF16),
            pltpu.VMEM((pairs, max(nx - 1, 1), 2, xrows, 128), BF16),
            pltpu.VMEM((layers, xrows, 128), BF16),
            pltpu.VMEM((pairs, max(nz - 1, 1), 2, zrows, 128), BF16),
            pltpu.VMEM((2 * layers, SUB, 128), F32),
            pltpu.VMEM((2 * layers, SUB, 128), BF16),
            pltpu.VMEM((layers, zrows, 128), F32),
            pltpu.VMEM((2, 2, grain, 128), F32),
            dma((3,)),
            dma, dma,
            dma, dma((pairs,)), dma, dma((pairs,)), dma, dma((pairs,)),
            dma((2,)), dma((2,)), dma((2,)), dma((2,)), dma((pairs,)), dma((pairs,)),
            dma((pairs,)), dma((pairs,)),
            dma, dma((layers,)), dma, dma((pairs,)), dma, dma((pairs,)),
            dma, dma,
        ],
        compiler_params=pltpu.CompilerParams(
            collective_id=0, has_side_effects=True, vmem_limit_bytes=60 * 2**20
        ),
        cost_estimate=pl.CostEstimate(
            flops=24 * layers * rows * local * 256,
            bytes_accessed=4 * rows * width,
            transcendentals=layers * rows * rows,
        ),
    )(inputs, cotangent, doc_lengths[:, 0, :], wg)
    full = jnp.concatenate([sums[0], sums[1]], axis=1)
    return ((full[:, :192] * gain)[None], full[:, 192:].T[None])


def solution(mesh, nx=4, nz=8):
    nc = mesh.shape["section"] // 2
    return jax.shard_map(
        functools.partial(body, nc, nx, nz),
        mesh=mesh,
        in_specs=(
            P(None, "dp", None),
            P(None, "dp", None),
            P(None, "dp", None),
            P("section", None),
            P("section", "dp", None),
            P("section", None, "dp"),
        ),
        out_specs=(P("section", "dp", None), P("section", None, "dp")),
        check_vma=False,
    )
```

```python
import functools

import jax
import jax.numpy as jnp
from jax import lax
from jax.experimental import pallas as pl
from jax.experimental.pallas import tpu as pltpu
from jax.sharding import PartitionSpec as P

MESH = pl.DeviceIdType.MESH
F32, BF16 = jnp.float32, jnp.bfloat16
SUB = 16


def nn(a, b):
    return jnp.dot(a, b, preferred_element_type=F32)


def nt(a, b):
    return lax.dot_general(a, b, (((1,), (1,)), ((), ())), preferred_element_type=F32)


def tn(a, b):
    return lax.dot_general(a, b, (((0,), (0,)), ((), ())), preferred_element_type=F32)


def kernel(
    nc, nx, nz, rows,
    inp, cot, lens, wg, out,
    W, xin, cin, X, DY, QK, KK, VV, PR, ATT, SC, SD, GM, UA,
    es, er, bs, br, gs, gr, G, SR, H, XR, H2, ZR, TALLY, TALLYB, FS, OB,
    in_sem, s1_s, s1_r, z_s, z_r, x_s, x_r, c_s, c_r,
    e_s, e_r, b_s, b_r, g_s, g_r, h_s, h_r, rc_s, rc_r, rx_s, rx_r, rz_s, rz_r, f_s, f_r,
):
    layers, pairs = 2 * nc, nc
    dps = nx * nz * 2
    local = SUB * dps
    width = local * nc
    zrows, xrows = 2 * SUB, 2 * SUB * nz
    s, d = lax.axis_index("section"), lax.axis_index("dp")
    c, k = lax.div(s, 2), lax.rem(s, 2)
    x, z, y = lax.div(d, 2 * nz), lax.rem(lax.div(d, 2), nz), lax.rem(d, 2)

    def at(start, size):
        return pl.ds(pl.multiple_of(start, SUB), size)

    def two(m):
        return pl.ds(2 * m, 2)

    def dp_of(px, pz, py):
        return (px * nz + pz) * 2 + py

    def far_first(n):
        return sorted(range(1, n), key=lambda o: -min(o, n - o))

    def column_peer(o):
        n = lax.rem(y * layers + s + o, 2 * layers)
        return lax.rem(n, layers), lax.div(n, layers)

    def chip_peer(o):
        return (2 * lax.rem(c + o, nc) + k, d)

    def x_peer(o):
        return lax.rem(x + o, nx)

    def z_peer(o):
        return lax.rem(z + o, nz)

    sibling = (2 * c + 1 - k, d)

    def send(src, dst, send_sem, recv_sem, device):
        pltpu.make_async_remote_copy(
            src_ref=src, dst_ref=dst, send_sem=send_sem, recv_sem=recv_sem,
            device_id=device, device_id_type=MESH,
        ).start()

    def wait(ref, sem):
        pltpu.make_async_copy(ref, ref, sem).wait()

    load_x = pltpu.make_async_copy(inp.at[k], xin, in_sem.at[0])
    load_c = pltpu.make_async_copy(cot.at[k], cin, in_sem.at[1])
    own = pltpu.make_async_copy(
        wg.at[k, at(SUB * c, SUB)], W.at[k, s, at(SUB * d, SUB)], in_sem.at[2]
    )
    load_x.start()
    load_c.start()
    own.start()

    barrier = pltpu.get_barrier_semaphore()
    peers = []
    for o in range(1, 2 * layers):
        t, ty = column_peer(o)
        peers += [(t, dp_of(x, z, ty))]
    peers += [(s, dp_of(x_peer(o), z, y)) for o in range(1, nx)]
    peers += [(s, dp_of(x, z_peer(o), y)) for o in range(1, nz)]
    for peer in peers:
        pl.semaphore_signal(barrier, inc=1, device_id=peer, device_id_type=MESH)
    grain = min(8, dps)
    big, small = grain * SUB * nc, grain * SUB
    at_row = lax.broadcasted_iota(jnp.int32, (big, small), 0)
    at_lane = lax.broadcasted_iota(jnp.int32, (big, small), 1)
    inside = at_lane & (SUB - 1)
    wanted = (at_lane - inside) * nc + inside + SUB * c
    pick = jnp.where(at_row == wanted, 1.0, 0.0).astype(BF16)

    def picked(source, m):
        return nn(source[:, m * big : (m + 1) * big], pick).astype(BF16)

    load_x.wait()
    for m in range(dps // grain):
        X[0, :, m * small : (m + 1) * small] = picked(xin, m)

    pl.semaphore_wait(barrier, len(peers))

    for o in range(1, 2 * layers):
        t, ty = column_peer(o)
        tc, tk = lax.div(t, 2), lax.rem(t, 2)
        send(
            wg.at[tk, at(SUB * tc, SUB)], W.at[tk, s, at(SUB * d, SUB)],
            s1_s, s1_r, (t, dp_of(x, z, ty)),
        )

    own.wait()
    columns = TALLYB.at[pl.ds(0, 2 * layers - 1)]
    wait(columns, s1_r)

    def z_gather(m):
        block = W.at[k, two(m), at(zrows * (x * nz + z), zrows)]
        for o in far_first(nz):
            send(block, block, z_s, z_r.at[m], (s, dp_of(x, z_peer(o), y)))

    def z_arrived(m):
        if nz > 1:
            wait(W.at[0, pl.ds(0, 2), pl.ds(0, zrows * (nz - 1))], z_r.at[m])

    def x_gather(m):
        block = W.at[k, two(m), at(xrows * x, xrows)]
        for o in far_first(nx):
            send(block, block, x_s, x_r.at[m], (s, dp_of(x_peer(o), z, y)))

    def x_arrived(m):
        if nx > 1:
            wait(W.at[0, pl.ds(0, 2), pl.ds(0, xrows * (nx - 1))], x_r.at[m])

    def core_gather(m):
        block = W.at[k, two(m)]
        send(block, block, c_s, c_r.at[m], sibling)

    half = at(32 * k, 32)

    def gamma(m):
        a, b = 2 * m, 2 * m + 1
        right = jnp.concatenate([W[0, b], W[1, b], W[1, a]], axis=1)
        part = tn(W[1, a], right)[64:]
        gs[m] = part.astype(BF16)
        for o in far_first(nc):
            send(gs.at[m, half], gr.at[m, o - 1], g_s.at[m], g_r.at[m], chip_peer(o))

    def gamma_sum(m):
        total = gs[m, half].astype(F32)
        if nc > 1:
            wait(gr.at[m], g_r.at[m])
            for o in range(nc - 1):
                total = total + gr[m, o].astype(F32)
            wait(gr.at[m], g_s.at[m])
        GM[m, :64] = jnp.zeros((64, 384), BF16)
        mine = GM.at[m, at(64 + 32 * k, 32)]
        mine[...] = total.astype(BF16)
        send(mine, mine, h_s.at[m], h_r.at[m], sibling)

    def gamma_arrived(m):
        wait(GM.at[m, pl.ds(64, 32)], h_r.at[m])
        wait(GM.at[m, pl.ds(64, 32)], h_s.at[m])

    row = lax.broadcasted_iota(jnp.int32, (rows, rows), 0)
    col = lax.broadcasted_iota(jnp.int32, (rows, rows), 1)
    first = lens[k, 0]
    allowed = ((row < first) == (col < first)) & (row >= col)
    lane = lax.broadcasted_iota(jnp.int32, (rows, 128), 1)
    low = lane < 64

    def both(l):
        return jnp.concatenate([W[0, l], W[1, l]], axis=1)

    def attend(l, t0, t1, square):
        scale = lax.rsqrt(square * (1.0 / width) + 1e-05)
        q = t0 * scale
        kk = pltpu.roll(q, 64, 1).astype(BF16)
        vv = pltpu.roll(jnp.where(low, t1 * scale, 0.0), 64, 1).astype(BF16)
        scores = nt(jnp.where(low, q, 0.0).astype(BF16), kk) * 0.125
        scores = jnp.where(allowed, scores, -1e30)
        top = jnp.max(scores, axis=1, keepdims=True)
        e = jnp.exp(scores - top)
        p = e / jnp.sum(e, axis=1, keepdims=True)
        att = nn(p.astype(BF16), vv).astype(BF16)
        QK[l] = q.astype(BF16)
        KK[l] = kk
        VV[l] = vv
        PR[l] = p
        ATT[l] = att
        SC[l] = jnp.broadcast_to(scale, (rows, 128))
        return att

    def forward(m):
        slot = lax.rem(m, 2)
        a, b = 2 * m, 2 * m + 1
        wait(W.at[0, pl.ds(0, 2)], c_r.at[m])
        xb = X[a]
        part = nn(xb, jnp.concatenate([both(a), both(b)], axis=1))
        wide = xb.astype(F32)
        square = jnp.sum(wide * wide, axis=1, keepdims=True)
        upper = square.astype(BF16).astype(F32)
        es[slot, :, :384] = part[:, :384].astype(BF16)
        tail = jnp.where(lane < 96, upper, square - upper)
        es[slot, :, 384:] = jnp.where(low, part[:, 384:], tail).astype(BF16)
        for o in far_first(nc):
            send(es.at[slot], er.at[slot, o - 1], e_s.at[slot], e_r.at[slot], chip_peer(o))
        gamma(m)
        between(m)
        t = [part[:, 128 * i : 128 * (i + 1)] for i in range(4)]
        if nc > 1:
            wait(er.at[slot], e_r.at[slot])
            for o in range(nc - 1):
                for i in range(4):
                    t[i] = t[i] + er[slot, o, :, 128 * i : 128 * (i + 1)].astype(F32)
                more = er[slot, o, :, 384:].astype(F32)
                square = square + more[:, 64:65] + more[:, 96:97]
            wait(er.at[slot], e_s.at[slot])
        gamma_sum(m)
        att = attend(a, t[0], t[1], square)

        @pl.when(m + 1 < pairs)
        def _():
            x_arrived(m + 1)
            core_gather(m + 1)

        gamma_arrived(m)
        u = nn(att, GM[m])
        into = jnp.where(low, 0.0, t[1])
        after = into + jnp.where(low, 0.0, u[:, 256:])
        UA[m] = after
        square = square + jnp.sum(att.astype(F32) * (into + after), axis=1, keepdims=True)
        last = attend(b, t[2] + u[:, :128], t[3] + u[:, 128:256], square)
        middle = (X[a].astype(F32) + nt(att, W[1, a])).astype(BF16)
        X[b] = middle

        @pl.when(m < pairs - 1)
        def _():
            X[b + 1] = (middle.astype(F32) + nt(last, W[1, b])).astype(BF16)

    def between(m):
        @pl.when(m + 2 < pairs)
        def _():
            z_arrived(m + 2)
            x_gather(m + 2)

        @pl.when(m + 3 < pairs)
        def _():
            z_gather(m + 3)

    z_gather(0)
    load_c.wait()
    for m in range(dps // grain):
        DY[layers - 1, :, m * small : (m + 1) * small] = picked(cin, m)
    z_arrived(0)
    x_gather(0)
    if pairs > 1:
        z_gather(1)
        z_arrived(1)
        x_gather(1)
    if pairs > 2:
        z_gather(2)
    x_arrived(0)
    core_gather(0)
    def forward_step(m, carry):
        forward(m)
        return carry

    lax.fori_loop(0, pairs, forward_step, 0)

    def grads_of(l):
        left = jnp.concatenate([X[l], DY[l]], axis=0)
        att = ATT[l]
        right = jnp.concatenate(
            [
                jnp.concatenate([SD[l, 0], SD[l, 1]], axis=1),
                jnp.concatenate([jnp.zeros_like(att), att], axis=1),
            ],
            axis=0,
        )
        g = tn(left, right)
        G[0, l] = g[:, :128].astype(BF16)
        G[1, l] = g[:, 128:].astype(BF16)
        send(G.at[1 - k, l], SR.at[l], rc_s, rc_r.at[l], sibling)

    def scatter_of(m, i):
        l = 2 * m + i
        wait(SR.at[l], rc_r.at[l])
        H[l] = (G[k, l].astype(F32) + SR[l].astype(F32)).astype(BF16)
        for o in far_first(nx):
            px = x_peer(o)
            send(
                H.at[l, at(xrows * px, xrows)], XR.at[m, o - 1, i],
                rx_s, rx_r.at[m], (s, dp_of(px, z, y)),
            )

    def grads(m):
        @pl.when(m > 0)
        def _():
            grads_of(2 * m + 1)

        grads_of(2 * m)

    def x_scatter(m):
        @pl.when(m > 0)
        def _():
            scatter_of(m, 1)

        scatter_of(m, 0)

    def z_scatter(m):
        total = H[two(m), at(xrows * x, xrows)].astype(F32)
        if nx > 1:
            wait(XR.at[m], rx_r.at[m])
            for o in range(nx - 1):
                total = total + XR[m, o].astype(F32)
        H2[two(m)] = total.astype(BF16)
        for o in far_first(nz):
            pz = z_peer(o)
            send(
                H2.at[two(m), at(zrows * pz, zrows)], ZR.at[m, o - 1],
                rz_s, rz_r.at[m], (s, dp_of(x, pz, y)),
            )

    def finish(m):
        total = H2[two(m), at(zrows * z, zrows)].astype(F32)
        if nz > 1:
            wait(ZR.at[m], rz_r.at[m])
            for o in range(nz - 1):
                total = total + ZR[m, o].astype(F32)
        FS[two(m)] = total
        for i in range(2):
            for ty in range(2):
                to_holder(2 * m + i, ty)

    def to_holder(l, ty):
        here = (l == s) & (y == ty)
        sums = FS.at[l, pl.ds(SUB * ty, SUB)]
        place = OB.at[y, k, at(SUB * c, SUB)]

        @pl.when(here)
        def _():
            place[...] = sums[...]

        @pl.when(jnp.logical_not(here))
        def _():
            send(sums, place, f_s, f_r, (l, dp_of(x, z, ty)))

    def staged(m, behind, stage):
        @pl.when((m + behind >= 0) & (m + behind < pairs))
        def _():
            stage(m + behind)

    def attend_back(l, da):
        da = jnp.where(low, 0.0, da).astype(BF16)
        vv, kk, p, scale = VV[l], KK[l], PR[l], SC[l]
        dp = nt(da, vv)
        ds = p * (dp - jnp.sum(p * dp, axis=1, keepdims=True)) * 0.125
        ds = ds.astype(BF16)
        dqk = jnp.where(low, nn(ds, kk), tn(ds, kk))
        dv = tn(p.astype(BF16), da)
        dot = dqk * QK[l].astype(F32) + dv * vv.astype(F32)
        dot = jnp.sum(dot, axis=1, keepdims=True)
        coef = scale[:, :1] * scale[:, :1] * dot * (1.0 / width)
        sd0 = (dqk * scale).astype(BF16)
        sd1 = (pltpu.roll(dv, 64, 1) * scale).astype(BF16)
        SD[l, 0] = sd0
        SD[l, 1] = sd1
        return jnp.concatenate([sd0, sd1], axis=1), coef

    def down(l, sd, coef):
        change = nt(sd, both(l)) - X[l].astype(F32) * coef
        DY[l - 1] = (DY[l].astype(F32) + change).astype(BF16)

    def backward_step(step, carry):
        m = pairs - 1 - step
        slot = lax.rem(step, 2)
        a, b = 2 * m, 2 * m + 1

        @pl.when(m >= 0)
        def _():
            part = nn(DY[b], jnp.concatenate([W[1, b], W[1, a]], axis=1))
            part = jnp.where(low, pltpu.roll(part[:, 128:], 64, 1), part[:, :128])
            bs[slot] = part.astype(BF16)
            for o in far_first(nc):
                send(bs.at[slot], br.at[slot, o - 1], b_s.at[slot], b_r.at[slot], chip_peer(o))

        staged(m, 1, grads)
        staged(m, 3, finish)
        staged(m, 1, x_scatter)
        staged(m, 2, z_scatter)

        @pl.when(m >= 0)
        def _():
            total = bs[slot].astype(F32)
            if nc > 1:
                wait(br.at[slot], b_r.at[slot])
                for o in range(nc - 1):
                    total = total + br[slot, o].astype(F32)
                wait(br.at[slot], b_s.at[slot])
            sd, coef = attend_back(b, total)
            other = nt(sd, GM[m, :, :256]) - UA[m] * coef
            down(b, sd, coef)

            @pl.when(m == 0)
            def _():
                grads_of(b)

            sd, coef = attend_back(a, pltpu.roll(total, 64, 1) + other)

            @pl.when(m == 0)
            def _():
                scatter_of(m, 1)

            @pl.when(m > 0)
            def _():
                down(a, sd, coef)

        return carry

    lax.fori_loop(0, pairs + 3, backward_step, 0)

    wait_f = TALLY.at[pl.ds(0, 2 * layers - 1)]
    wait(wait_f, f_r)
    out[...] = OB[0] + OB[1]

    wait(columns, s1_s)
    if nz > 1:
        for o in range(1, nz):
            wait(W.at[0, :, pl.ds(0, zrows)], z_s)
            wait(H2.at[:, pl.ds(0, zrows)], rz_s)
    if nx > 1:
        for o in range(1, nx):
            wait(W.at[0, :, pl.ds(0, xrows)], x_s)
            wait(H2, rx_s)
    wait(W.at[0], c_s)
    wait(H, rc_s)
    wait(wait_f, f_s)


def body(nc, nx, nz, inputs, cotangent, doc_lengths, norm_gain, w_qkv, w_out):
    rows, width = inputs.shape[1:]
    layers, pairs, dps = 2 * nc, nc, nx * nz * 2
    local = SUB * dps
    grain = SUB * nc
    d = lax.axis_index("dp")
    gain = lax.dynamic_slice(norm_gain[0], (d * grain,), (grain,)).astype(F32)[:, None]
    wq = (w_qkv[0].astype(F32) * gain).astype(BF16)
    wg = jnp.concatenate([wq, w_out[0].T], axis=1)
    wg = jnp.stack([wg[:, :128], wg[:, 128:]])
    vmem = pl.BlockSpec(memory_space=pltpu.VMEM)
    anywhere = pl.BlockSpec(memory_space=pl.ANY)
    dma = pltpu.SemaphoreType.DMA
    xrows, zrows = 2 * SUB * nz, 2 * SUB
    sums = pl.pallas_call(
        functools.partial(kernel, nc, nx, nz, rows),
        out_shape=jax.ShapeDtypeStruct((2, grain, 128), F32),
        in_specs=[anywhere, anywhere, pl.BlockSpec(memory_space=pltpu.SMEM), vmem],
        out_specs=vmem,
        scratch_shapes=[
            pltpu.VMEM((2, layers, local, 128), BF16),
            pltpu.VMEM((rows, width), BF16),
            pltpu.VMEM((rows, width), BF16),
            pltpu.VMEM((layers, rows, local), BF16),
            pltpu.VMEM((layers, rows, local), BF16),
            pltpu.VMEM((layers, rows, 128), BF16),
            pltpu.VMEM((layers, rows, 128), BF16),
            pltpu.VMEM((layers, rows, 128), BF16),
            pltpu.VMEM((layers, rows, rows), F32),
            pltpu.VMEM((layers, rows, 128), BF16),
            pltpu.VMEM((layers, rows, 128), F32),
            pltpu.VMEM((layers, 2, rows, 128), BF16),
            pltpu.VMEM((pairs, 128, 384), BF16),
            pltpu.VMEM((pairs, rows, 128), F32),
            pltpu.VMEM((2, rows, 512), BF16),
            pltpu.VMEM((2, max(nc - 1, 1), rows, 512), BF16),
            pltpu.VMEM((2, rows, 128), BF16),
            pltpu.VMEM((2, max(nc - 1, 1), rows, 128), BF16),
            pltpu.VMEM((pairs, 64, 384), BF16),
            pltpu.VMEM((pairs, max(nc - 1, 1), 32, 384), BF16),
            pltpu.VMEM((2, layers, local, 128), BF16),
            pltpu.VMEM((layers, local, 128), BF16),
            pltpu.VMEM((layers, local, 128), BF16),
            pltpu.VMEM((pairs, max(nx - 1, 1), 2, xrows, 128), BF16),
            pltpu.VMEM((layers, xrows, 128), BF16),
            pltpu.VMEM((pairs, max(nz - 1, 1), 2, zrows, 128), BF16),
            pltpu.VMEM((2 * layers, SUB, 128), F32),
            pltpu.VMEM((2 * layers, SUB, 128), BF16),
            pltpu.VMEM((layers, zrows, 128), F32),
            pltpu.VMEM((2, 2, grain, 128), F32),
            dma((3,)),
            dma, dma,
            dma, dma((pairs,)), dma, dma((pairs,)), dma, dma((pairs,)),
            dma((2,)), dma((2,)), dma((2,)), dma((2,)), dma((pairs,)), dma((pairs,)),
            dma((pairs,)), dma((pairs,)),
            dma, dma((layers,)), dma, dma((pairs,)), dma, dma((pairs,)),
            dma, dma,
        ],
        compiler_params=pltpu.CompilerParams(
            collective_id=0, has_side_effects=True, vmem_limit_bytes=60 * 2**20
        ),
        cost_estimate=pl.CostEstimate(
            flops=24 * layers * rows * local * 256,
            bytes_accessed=4 * rows * width,
            transcendentals=layers * rows * rows,
        ),
    )(inputs, cotangent, doc_lengths[:, 0, :], wg)
    full = jnp.concatenate([sums[0], sums[1]], axis=1)
    return ((full[:, :192] * gain)[None], full[:, 192:].T[None])


def solution(mesh, nx=4, nz=8):
    nc = mesh.shape["section"] // 2
    return jax.shard_map(
        functools.partial(body, nc, nx, nz),
        mesh=mesh,
        in_specs=(
            P(None, "dp", None),
            P(None, "dp", None),
            P(None, "dp", None),
            P("section", None),
            P("section", "dp", None),
            P("section", None, "dp"),
        ),
        out_specs=(P("section", "dp", None), P("section", None, "dp")),
        check_vma=False,
    )
```
